32 devices in a mesh: grp: 4 (over x, core), dp: 8 (over z, y).
Axes of the slice: x: 2, y: 2, z: 4, core: 2. Of those that a mesh axis runs over, the one named last changes fastest.
Arguments:
- images: float32 [2, 64, 3, 32, 32], P(None, ('grp', 'dp')), may hold values from -1 to 1
- noise: float32 [2, 64, 3, 32, 32], P(None, ('grp', 'dp')), may hold values from -4 to 4
- timesteps: int32 [2, 64], P(None, ('grp', 'dp')), may hold values from 16 to 64
- counts: int32 [32, 2], P(('grp', 'dp')), may hold values from 1 to 2, as said below
- teacher: bfloat16 [2239488], replicated
- params: float32 [2239488], replicated
- first_moment: float32 [4, 2239488], P('grp'), may hold values from -5.722046e-06 to 5.722046e-06
- second_moment: float32 [4, 2239488], P('grp'), may hold values from 5.581633e-15 to 8.9306126e-14
- outer_momentum: float32 [2239488], replicated, may hold values from -0.15625 to 0.15625
Outputs:
- new_weights: float32 [2239488], replicated
- new_first: float32 [4, 2239488], P('grp')
- new_second: float32 [4, 2239488], P('grp')
- average_diff: float32 [2239488], replicated
- new_outer: float32 [2239488], replicated
- loss_sum: float32 [4], P('grp')
- loss_count: float32 [4], P('grp')
- grad_norm: float32 [4], P('grp')
The draws below stay inside these ranges and needn't reach their ends.
Inputs may be any that keep to these rules, and one draw needn't show every extreme that they name: Slots 0 to counts - 1 of a device in a turn hold images; the others are ignored.
All inputs are finite; a program needn't handle non-finite values.
Results may differ from the reference program's by a relative error of at most 0.0083.
Values may be sent and summed in bfloat16 or wider, within the bound.
A program may use at most 512 MiB of HBM per device.

```python
import math
import jax
import jax.numpy as jnp
from jax import lax

BASE = 128
WIDE = 256
TEMB = 512
FREQ = 128
GROUPS = 32
SIDE = 32
IMG_DEV = 2
STEPS = 64
STEP_COUNT = 10
TURNS = 2
IMAGES = 64
NPARAM = 2239488
N_GRP = 4
N_DP = 8


def layout_drawn():
    return [('conv_in', (BASE, 3, 3, 3), 'weight', 27 ** (-0.5)), ('bias_in', (BASE,), 'bias', 0.3), ('conv_down', (WIDE, BASE, 3, 3), 'weight', (9 * BASE) ** (-0.5)), ('bias_down', (WIDE,), 'bias', 0.3), ('norm_one_gain', (WIDE,), 'gain', 1.0), ('norm_one_shift', (WIDE,), 'bias', 0.3), ('conv_one', (WIDE, WIDE, 3, 3), 'weight', (9 * WIDE) ** (-0.5)), ('bias_one', (WIDE,), 'bias', 0.3), ('time_one', (FREQ, TEMB), 'weight', FREQ ** (-0.5)), ('time_bias_one', (TEMB,), 'bias', 0.3), ('time_two', (TEMB, WIDE), 'weight', TEMB ** (-0.5)), ('time_bias_two', (WIDE,), 'bias', 0.3), ('norm_two_gain', (WIDE,), 'gain', 1.0), ('norm_two_shift', (WIDE,), 'bias', 0.3), ('conv_two', (WIDE, WIDE, 3, 3), 'weight', (9 * WIDE) ** (-0.5)), ('bias_two', (WIDE,), 'bias', 0.3), ('attn_gain', (WIDE,), 'gain', 1.0), ('attn_shift', (WIDE,), 'bias', 0.3), ('attn_inner', (WIDE, 3 * WIDE), 'weight', WIDE ** (-0.5)), ('attn_outer', (WIDE, WIDE), 'weight', max(WIDE // 64, 1) ** (-0.5)), ('attn_bias', (WIDE,), 'bias', 0.3), ('conv_up', (BASE, WIDE, 3, 3), 'weight', (9 * WIDE) ** (-0.5)), ('bias_up', (BASE,), 'bias', 0.3), ('norm_out_gain', (BASE,), 'gain', 1.0), ('norm_out_shift', (BASE,), 'bias', 0.3), ('conv_out', (3, BASE, 3, 3), 'weight', (9 * BASE) ** (-0.5)), ('bias_out', (3,), 'bias', 0.3)]


def flat_draw(key):
    segments = []
    used = 0
    for position, (entry_name, extent, category, spread) in enumerate(layout_drawn()):
        subkey = jax.random.fold_in(key, position)
        number = math.prod(extent)
        used += number
        if category == 'gain':
            ramp_up = 0.5 + jnp.arange(number, dtype=jnp.float32) / max(number - 1, 1)
            segments.append(ramp_up * jax.random.uniform(subkey, (number,), jnp.float32, 0.8, 1.25))
        else:
            gauss = jax.random.normal(subkey, (number,), jnp.float32)
            segments.append(spread * gauss)
    filler = NPARAM - used
    segments.append(0.02 * jax.random.normal(jax.random.fold_in(key, 999), (filler,), jnp.float32))
    return jnp.concatenate(segments)


def draw_params(key, part):
    key = jax.random.fold_in(key, 11)
    return flat_draw(key)


def draw_teacher(key, part):
    key = jax.random.fold_in(key, 12)
    return flat_draw(key).astype(jnp.bfloat16)


def draw_counts(key, part):
    key = jax.random.fold_in(key, 13)
    rows_all = N_GRP * N_DP
    lane = (jnp.arange(rows_all, dtype=jnp.int32) % N_DP)[:, None]
    denominator = 3 * (N_DP - 1)
    base_count = (IMG_DEV * (N_DP - 1 + 2 * lane) + denominator - 1) // denominator
    jitter = jax.random.randint(key, (rows_all, TURNS), -1, 1, dtype=jnp.int32)
    jitter = jitter * (lane < N_DP - 1).astype(jnp.int32)
    return jnp.clip(base_count + jitter, 1, IMG_DEV).astype(jnp.int32)


def touch_ends(values, stream_key, low, high):
    longest = values.shape.index(max(values.shape))
    spots = []
    for shift in (0, 1):
        where = [jax.random.randint(jax.random.fold_in(stream_key, axis), (), 0, length) for axis, length in enumerate(values.shape)]
        where[longest] = (where[longest] + shift) % values.shape[longest]
        spots.append(tuple(where))
    return values.at[spots[0]].set(low).at[spots[1]].set(high)


def steps_of(stream_key, dims, split, least, largest):
    def one(dim, shards_of):
        heights = jax.random.uniform(jax.random.fold_in(jax.random.fold_in(stream_key, 6), dim), (shards_of,), jnp.float32, least / len(split), largest / len(split))
        return jnp.repeat(jnp.exp(heights), dims[dim] // shards_of).reshape((-1,) + (1,) * (len(dims) - dim - 1))

    level = one(*split[0])
    for cut in split[1:]:
        level = level * one(*cut)
    return level


def centred(rng, shape, width, reach, pieces=(), held_as=jnp.bfloat16):
    level = steps_of(rng, shape, pieces, -0.22, 0.18) if pieces else 1.0
    entries = jax.random.normal(rng, shape, jnp.float32) * width * level
    return jnp.minimum(jnp.maximum(entries, -reach), reach).astype(held_as)


def setup_inputs(seed: int = 0) -> dict:
    streams_of = jax.random.split(jax.random.key(seed), 10)
    return {
        "images": jnp.clip(jax.random.uniform(streams_of[0], (TURNS, IMAGES, 3, SIDE, SIDE), jnp.float32, -1.0, 1.0) * steps_of(streams_of[0], (TURNS, IMAGES, 3, SIDE, SIDE), ((1, 32),), -0.4, 0.0), -1.0, 1.0),
        "noise": centred(streams_of[1], (TURNS, IMAGES, 3, SIDE, SIDE), 1.0, 4.0, ((1, 32),), jnp.float32),
        "timesteps": touch_ends(jax.random.randint(streams_of[2], (TURNS, IMAGES), STEPS // 4, STEPS + 1), jax.random.fold_in(streams_of[2], 1), STEPS // 4, STEPS).astype(jnp.int32),
        "counts": draw_counts(jax.random.fold_in(streams_of[9], 71), 0),
        "teacher": draw_teacher(jax.random.fold_in(streams_of[9], 71), 0),
        "params": draw_params(jax.random.fold_in(streams_of[9], 71), 0),
        "first_moment": centred(streams_of[6], (N_GRP, NPARAM), (0.111 * 0.005 / NPARAM ** 0.5), 5.7220458984375e-06, ((0, 4),), jnp.float32),
        "second_moment": jnp.clip(jnp.exp(math.log(8.930612597091853e-14) - 2.7725887 * jax.random.uniform(streams_of[7], (N_GRP, NPARAM), jnp.float32) ** steps_of(streams_of[7], (N_GRP, NPARAM), ((0, 4),), -0.2, 0.2)), 5.581632873182408e-15, 8.930612597091853e-14),
        "outer_momentum": centred(streams_of[8], (NPARAM,), 0.01, 0.15625, (), jnp.float32),
    }


BETA_ONE = 0.9
BETA_TWO = 0.999
EPSILON = 1e-08
RATE_INNER = 0.03
WEIGHT_DECAY = 0.01
CLIP_NORM = 0.005
OUTER_RATE = 0.7
MOMENTUM_OUTER = 0.9

@jax.custom_vjp
def low(v):
    return lax.optimization_barrier(v.astype(jnp.bfloat16)).astype(jnp.float32)

@jax.custom_vjp
def low_back(v):
    return v

def low_keep(v):
    return (low(v), None)

def low_pass(kept, grad):
    return (grad,)

def back_keep(v):
    return (v, None)

def back_low(kept, grad):
    return (low(grad),)
low.defvjp(low_keep, low_pass)
low_back.defvjp(back_keep, back_low)

def layout():
    return [('conv_in', (BASE, 3, 3, 3), 'weight'), ('bias_in', (BASE,), 'bias'), ('conv_down', (WIDE, BASE, 3, 3), 'weight'), ('bias_down', (WIDE,), 'bias'), ('norm_one_gain', (WIDE,), 'gain'), ('norm_one_shift', (WIDE,), 'bias'), ('conv_one', (WIDE, WIDE, 3, 3), 'weight'), ('bias_one', (WIDE,), 'bias'), ('time_one', (FREQ, TEMB), 'weight'), ('time_bias_one', (TEMB,), 'bias'), ('time_two', (TEMB, WIDE), 'weight'), ('time_bias_two', (WIDE,), 'bias'), ('norm_two_gain', (WIDE,), 'gain'), ('norm_two_shift', (WIDE,), 'bias'), ('conv_two', (WIDE, WIDE, 3, 3), 'weight'), ('bias_two', (WIDE,), 'bias'), ('attn_gain', (WIDE,), 'gain'), ('attn_shift', (WIDE,), 'bias'), ('attn_inner', (WIDE, 3 * WIDE), 'weight'), ('attn_outer', (WIDE, WIDE), 'weight'), ('attn_bias', (WIDE,), 'bias'), ('conv_up', (BASE, WIDE, 3, 3), 'weight'), ('bias_up', (BASE,), 'bias'), ('norm_out_gain', (BASE,), 'gain'), ('norm_out_shift', (BASE,), 'bias'), ('conv_out', (3, BASE, 3, 3), 'weight'), ('bias_out', (3,), 'bias')]

def unpack(flat_weights):
    found = {}
    offset = 0
    for entry_name, extent, category in layout():
        number = math.prod(extent)
        segment = flat_weights[offset:offset + number].reshape(extent)
        found[entry_name] = low(segment) if category == 'weight' else segment
        offset += number
    return found

def group_norm(values, gain, shift):
    grouped = values.reshape(values.shape[0], GROUPS, -1)
    centered = grouped - lax.optimization_barrier(jnp.mean(grouped, axis=2, keepdims=True))
    normed = centered * lax.rsqrt(lax.optimization_barrier(jnp.mean(centered * centered, axis=2, keepdims=True)) + 1e-05)
    return normed.reshape(values.shape) * gain[None, :, None, None] + shift[None, :, None, None]

def convolve(activation, kernel, stride, precision):
    result = lax.conv_general_dilated(low(activation), kernel, (stride, stride), ((1, 1), (1, 1)), dimension_numbers=('NCHW', 'OIHW', 'NCHW'), precision=precision)
    return low_back(result)

def project(activation, matrix, precision):
    return low_back(jnp.dot(low(activation), matrix, precision=precision))

def column(vector):
    return vector[None, :, None, None]

def attend(middle, found, precision):
    images_here, channels, height_px, width_px = middle.shape
    normed = group_norm(middle, found['attn_gain'], found['attn_shift'])
    tokens_in = normed.reshape(images_here, channels, height_px * width_px).transpose(0, 2, 1)
    joined = project(tokens_in, found['attn_inner'], precision)
    query_rows = joined[..., :channels]
    key_rows = joined[..., channels:2 * channels]
    value_rows = joined[..., 2 * channels:]
    scores = low_back(jnp.einsum('nqc,nkc->nqk', low(query_rows), low(key_rows), precision=precision) * channels ** (-0.5))
    weights_soft = jax.nn.softmax(scores, axis=-1)
    mixed = low_back(jnp.einsum('nqk,nkc->nqc', low(weights_soft), low(value_rows), precision=precision))
    result = project(mixed, found['attn_outer'], precision) + found['attn_bias']
    return result.transpose(0, 2, 1).reshape(middle.shape)

def denoise(flat_weights, noisy, times_now, precision):
    found = unpack(flat_weights)
    half_freq = FREQ // 2
    freqs = jnp.exp(-math.log(10000.0) * jnp.arange(half_freq).astype(times_now.dtype) / (half_freq - 1))
    angles = 1000.0 * times_now[:, None] * freqs[None, :]
    embed = jnp.concatenate([jnp.sin(angles), jnp.cos(angles)], axis=1)
    hidden_time = jax.nn.silu(project(embed, found['time_one'], precision) + found['time_bias_one'])
    time_shift = project(hidden_time, found['time_two'], precision) + found['time_bias_two']
    first = convolve(noisy, found['conv_in'], 1, precision) + column(found['bias_in'])
    down = convolve(first, found['conv_down'], 2, precision) + column(found['bias_down'])
    branch = jax.nn.silu(group_norm(down, found['norm_one_gain'], found['norm_one_shift']))
    branch = convolve(branch, found['conv_one'], 1, precision) + column(found['bias_one']) + time_shift[:, :, None, None]
    branch = jax.nn.silu(group_norm(branch, found['norm_two_gain'], found['norm_two_shift']))
    middle = down + convolve(branch, found['conv_two'], 1, precision) + column(found['bias_two'])
    middle = middle + attend(middle, found, precision)
    upsampled = jnp.repeat(jnp.repeat(middle, 2, axis=2), 2, axis=3)
    upper = convolve(upsampled, found['conv_up'], 1, precision) + column(found['bias_up']) + first
    ending = jax.nn.silu(group_norm(upper, found['norm_out_gain'], found['norm_out_shift']))
    return convolve(ending, found['conv_out'], 1, precision) + column(found['bias_out'])

def plan(times_now):
    return (jnp.cos(0.5 * math.pi * times_now)[:, None, None, None], jnp.sin(0.5 * math.pi * times_now)[:, None, None, None])

def distill_target(teacher_flat, noisy, times_now, precision):
    times_mid = times_now - 0.5 / STEPS
    times_end = times_now - 1.0 / STEPS
    alpha_now, sigma_now = plan(times_now)
    alpha_mid, sigma_mid = plan(times_mid)
    alpha_end, sigma_end = plan(times_end)
    guess_one = denoise(teacher_flat, noisy, times_now, precision)
    middle_state = alpha_mid * guess_one + sigma_mid * (noisy - alpha_now * guess_one) / sigma_now
    guess_two = denoise(teacher_flat, middle_state, times_mid, precision)
    end_state = alpha_end * guess_two + sigma_end * (middle_state - alpha_mid * guess_two) / sigma_mid
    ratio = sigma_end / sigma_now
    return (end_state - ratio * noisy) / (alpha_end - ratio * alpha_now)

def snr_weight(times_now):
    alpha_now, sigma_now = plan(times_now)
    return (1.0 + (alpha_now / sigma_now) ** 2)[:, 0, 0, 0]

def student_loss(flat_weights, noisy, times_now, target, weighting, precision):
    guess = denoise(flat_weights, noisy, times_now, precision)
    error = lax.optimization_barrier(jnp.mean((guess - target) ** 2, axis=(1, 2, 3)))
    return jnp.sum(error * weighting)

def adamw_update(gradient_sum, valid_total, square_total, start, first, second):
    norm_value = jnp.sqrt(square_total) / valid_total
    factor = CLIP_NORM / jnp.maximum(norm_value, CLIP_NORM) / valid_total
    clipped = gradient_sum * factor
    new_first = BETA_ONE * first + (1.0 - BETA_ONE) * clipped
    new_second = BETA_TWO * second + (1.0 - BETA_TWO) * clipped * clipped
    corrected = new_first / (1.0 - BETA_ONE ** STEP_COUNT) / (jnp.sqrt(new_second / (1.0 - BETA_TWO ** STEP_COUNT)) + EPSILON)
    return (RATE_INNER * (corrected + WEIGHT_DECAY * start), new_first, new_second, norm_value)

def outer_step(average, start, momentum):
    new_momentum = MOMENTUM_OUTER * momentum + average
    return (start - OUTER_RATE * (average + MOMENTUM_OUTER * new_momentum), new_momentum)

def reference(images, noise, timesteps, counts, teacher, params, first_moment, second_moment, outer_momentum):
    teacher_flat = teacher.astype(jnp.float32)
    highest = lax.Precision.HIGHEST
    image_shape = (3, SIDE, SIDE)
    image_grid = images.reshape((TURNS, N_GRP, N_DP, IMG_DEV) + image_shape)
    noise_grid = noise.reshape((TURNS, N_GRP, N_DP, IMG_DEV) + image_shape)
    time_grid = timesteps.reshape(TURNS, N_GRP, N_DP, IMG_DEV)
    count_grid = counts.reshape(N_GRP, N_DP, TURNS)
    slot_index = jnp.arange(IMG_DEV).astype(jnp.int32)

    def accumulate(carry, block_data):
        clean, fresh, steps_int, valid_num = block_data
        times_now = steps_int.astype(params.dtype) / STEPS
        alpha_now, sigma_now = plan(times_now)
        noisy = low(alpha_now * clean + sigma_now * fresh)
        target = distill_target(teacher_flat, noisy, times_now, highest)
        valid = (slot_index < valid_num).astype(params.dtype)
        weighting = valid * snr_weight(times_now)
        loss_value, pullback = jax.vjp(lambda flat_now: student_loss(flat_now, noisy, times_now, target, weighting, highest), params)
        gradient = pullback(jnp.ones((), params.dtype))[0]
        return ((carry[0] + gradient, carry[1] + loss_value, carry[2] + jnp.sum(valid)), None)
    diff_total = jnp.zeros_like(params)
    firsts, seconds, losses, totals, norms = ([], [], [], [], [])
    for group_index in range(N_GRP):
        blocks = (image_grid[:, group_index].reshape((TURNS * N_DP, IMG_DEV) + image_shape), noise_grid[:, group_index].reshape((TURNS * N_DP, IMG_DEV) + image_shape), time_grid[:, group_index].reshape(TURNS * N_DP, IMG_DEV), count_grid[group_index].T.reshape(TURNS * N_DP))
        start_carry = (jnp.zeros_like(params), jnp.zeros((), params.dtype), jnp.zeros((), params.dtype))
        (gradient_sum, loss_total, valid_total), _ = lax.scan(accumulate, start_carry, blocks)
        square_total = jnp.sum(gradient_sum * gradient_sum)
        diff, new_first, new_second, norm_value = adamw_update(gradient_sum, valid_total, square_total, params, first_moment[group_index], second_moment[group_index])
        diff_total = diff_total + diff
        firsts.append(new_first)
        seconds.append(new_second)
        losses.append(loss_total)
        totals.append(valid_total)
        norms.append(norm_value)
    average = diff_total / N_GRP
    new_weights, new_outer = outer_step(average, params, outer_momentum)
    return (new_weights, jnp.stack(firsts), jnp.stack(seconds), average, new_outer, jnp.stack(losses), jnp.stack(totals), jnp.stack(norms))
```

```python
import math
from types import SimpleNamespace

import jax
import jax.numpy as jnp
from jax import lax
from jax.experimental import pallas as pl
from jax.experimental.pallas import tpu as pltpu
from jax.sharding import PartitionSpec as P

BASE = 128
WIDE = 256
TEMB = 512
FREQ = 128
GROUPS = 32
STEPS = 64
STEP_COUNT = 10

BETA_ONE = 0.9
BETA_TWO = 0.999
EPSILON = 1e-08
RATE_INNER = 0.03
WEIGHT_DECAY = 0.01
CLIP_NORM = 0.005
OUTER_RATE = 0.7
MOMENTUM_OUTER = 0.9

F32 = jnp.float32
BF16 = jnp.bfloat16
LANES = 128
HALF = 16
PIX = HALF * HALF
VMEM_LIMIT = 60 * 1024 * 1024
MESH = pl.DeviceIdType.MESH
PIECES = 5
UNIT = 320
LOSS_GAP = 8


SIZES = dict(
    conv_in=BASE * 27,
    bias_in=BASE,
    conv_down=WIDE * BASE * 9,
    bias_down=WIDE,
    norm_one_gain=WIDE,
    norm_one_shift=WIDE,
    conv_one=WIDE * WIDE * 9,
    bias_one=WIDE,
    time_one=FREQ * TEMB,
    time_bias_one=TEMB,
    time_two=TEMB * WIDE,
    time_bias_two=WIDE,
    norm_two_gain=WIDE,
    norm_two_shift=WIDE,
    conv_two=WIDE * WIDE * 9,
    bias_two=WIDE,
    attn_gain=WIDE,
    attn_shift=WIDE,
    attn_inner=WIDE * 3 * WIDE,
    attn_outer=WIDE * WIDE,
    attn_bias=WIDE,
    conv_up=BASE * WIDE * 9,
    bias_up=BASE,
    norm_out_gain=BASE,
    norm_out_shift=BASE,
    conv_out=3 * BASE * 9,
    bias_out=3,
)


def layout():
    return list(SIZES.items())


def start_rows():
    found = {}
    offset = 0
    for name, number in layout():
        found[name] = offset // LANES
        offset += number
    return SimpleNamespace(**found)


ROW = start_rows()
VECTOR_PLACES = dict(
    bias_in=0,
    bias_down=1,
    norm_one_gain=2,
    norm_one_shift=3,
    bias_one=4,
    time_bias_two=5,
    norm_two_gain=6,
    norm_two_shift=7,
    bias_two=8,
    attn_gain=9,
    attn_shift=10,
    attn_bias=11,
    bias_up=12,
    norm_out_gain=13,
    norm_out_shift=14,
)
VEC = SimpleNamespace(**VECTOR_PLACES)
VECTORS = [(place, getattr(ROW, name), SIZES[name] == BASE) for name, place in VECTOR_PLACES.items()]
JOINT = {(0, 0): (0,), (0, 1): (1, 2), (1, 0): (0, 1), (1, 1): (2,)}

PREP_SHAPES = dict(
    down=(3, 3 * BASE, WIDE),
    one=(3, 3 * WIDE, WIDE),
    two=(3, 3 * WIDE, WIDE),
    inner=(WIDE, 3 * WIDE),
    outer=(WIDE, WIDE),
    up=(4, 3 * WIDE, WIDE),
    time_one=(FREQ, TEMB),
    time_two=(TEMB, WIDE),
)
BACK_SHAPES = dict(
    down_t=(3, 2 * WIDE, WIDE),
    one_t=(3, 3 * WIDE, WIDE),
    two_t=(3, 3 * WIDE, WIDE),
    inner_t=(3 * WIDE, WIDE),
    outer_t=(WIDE, WIDE),
    up_t=(4, 2 * WIDE, WIDE),
    time_two_t=(WIDE, TEMB),
)


def dot(a, b):
    return jnp.dot(a, b, preferred_element_type=F32)


def narrow_places():
    begin = 27 * lax.broadcasted_iota(jnp.int32, (32, LANES), 1)
    row = lax.broadcasted_iota(jnp.int32, (32, LANES), 0)
    low = jnp.where(begin // LANES == row, 1.0, 0.0)
    high = jnp.where(begin // LANES + 1 == row, 1.0, 0.0)
    offset = (27 * lax.broadcasted_iota(jnp.int32, (LANES, LANES), 0)) % LANES
    lane = lax.broadcasted_iota(jnp.int32, (LANES, LANES), 1)
    return low, high, offset, lane >= offset


def roll_rows(values, offset, sign):
    for bit in range(7):
        moved = pltpu.roll(values, (sign << bit) % LANES, axis=1)
        values = jnp.where((offset >> bit) % 2 == 1, moved, values)
    return values


def prep_kernel(with_back, rows, *refs):
    names = list(PREP_SHAPES) + (list(BACK_SHAPES) if with_back else [])
    out = SimpleNamespace(**dict(zip(names, refs)))
    enter, leave, bias_out, vec, bias_hidden, turned, square, taps = refs[len(names) :]

    def turn(start, wide_out, wide_in):
        count = wide_in * 9 // LANES
        for b in range(count):
            block = rows[pl.ds(start + b, wide_out, stride=count), :].T
            for c in range(0, wide_out, LANES):
                turned[c // LANES, b * LANES : (b + 1) * LANES, :] = block[:, c : c + LANES]

    def tap(k, wide_out, wide_in):
        parts = [turned[c, pl.ds(k, wide_in, stride=9), :] for c in range(wide_out // LANES)]
        return parts[0] if len(parts) == 1 else jnp.concatenate(parts, axis=1)

    for start, place, place_t in (
        (ROW.conv_one, out.one, out.one_t if with_back else None),
        (ROW.conv_two, out.two, out.two_t if with_back else None),
    ):
        turn(start, WIDE, WIDE)
        for ky in range(3):
            for kx in range(3):
                block = tap(3 * ky + kx, WIDE, WIDE)
                place[ky, kx * WIDE : (kx + 1) * WIDE, :] = block.astype(BF16)
                if with_back:
                    place_t[ky, kx * WIDE : (kx + 1) * WIDE, :] = block.T.astype(BF16)
    turn(ROW.conv_down, WIDE, BASE)
    for ky in range(3):
        for kx in range(3):
            block = tap(3 * ky + kx, WIDE, BASE)
            out.down[ky, kx * BASE : (kx + 1) * BASE, :] = block.astype(BF16)
            if with_back:
                back = block.T.astype(BF16)
                if kx == 0:
                    out.down_t[ky, 0:WIDE, BASE:] = back
                elif kx == 1:
                    out.down_t[ky, 0:WIDE, 0:BASE] = jnp.zeros((WIDE, BASE), BF16)
                    out.down_t[ky, WIDE:, 0:BASE] = back
                else:
                    out.down_t[ky, WIDE:, BASE:] = back
    turn(ROW.conv_up, BASE, WIDE)
    for py in range(2):
        for ty in range(2):
            index = 2 * py + ty
            for px in range(2):
                for tx in range(2):
                    total = None
                    for ky in JOINT[py, ty]:
                        for kx in JOINT[px, tx]:
                            term = tap(3 * ky + kx, BASE, WIDE).astype(BF16).astype(F32)
                            total = term if total is None else total + term
                    xo = px + tx
                    out.up[index, xo * WIDE : (xo + 1) * WIDE, px * BASE : (px + 1) * BASE] = (
                        total.astype(BF16)
                    )
                    if with_back:
                        at = (2 * px + tx) * BASE
                        out.up_t[index, at : at + BASE, :] = total.T.astype(BF16)
                at = 2 * WIDE if px == 0 else 0
                out.up[index, at : at + WIDE, px * BASE : (px + 1) * BASE] = jnp.zeros(
                    (WIDE, BASE), BF16
                )
    for start, place, place_t in (
        (ROW.attn_inner, out.inner, out.inner_t if with_back else None),
        (ROW.attn_outer, out.outer, out.outer_t if with_back else None),
        (ROW.time_one, out.time_one, None),
        (ROW.time_two, out.time_two, out.time_two_t if with_back else None),
    ):
        height, width = place.shape
        count = width // LANES
        for b in range(count):
            block = rows[pl.ds(start + b, height, stride=count), :]
            place[:, b * LANES : (b + 1) * LANES] = block.astype(BF16)
            if place_t is not None:
                place_t[b * LANES : (b + 1) * LANES, :] = block.T.astype(BF16)
    vec[...] = jnp.zeros_like(vec)
    for place, r, narrow in VECTORS:
        second = r if narrow else r + 1
        vec[place : place + 1, 0:LANES] = rows[r : r + 1, :]
        vec[place : place + 1, LANES:] = rows[second : second + 1, :]
    for b in range(TEMB // LANES):
        r = ROW.time_bias_one + b
        bias_hidden[:, b * LANES : (b + 1) * LANES] = jnp.broadcast_to(rows[r : r + 1, :], (8, LANES))
    low, high, offset, upper_part = narrow_places()
    block = rows[0:32, :].astype(BF16)
    merged = jnp.where(
        upper_part, dot(low.T.astype(BF16), block), dot(high.T.astype(BF16), block)
    )
    merged = roll_rows(merged, offset, -1).T
    taps[...] = jnp.zeros_like(taps)
    for k in range(9):
        for c in range(3):
            taps[8 * k + c : 8 * k + c + 1, :] = merged[9 * c + k : 9 * c + k + 1, :]
    enter[...] = taps[...].astype(BF16)
    square[...] = jnp.zeros_like(square)
    for b in range(9):
        for c in range(3):
            at = ROW.conv_out + 9 * c + b
            square[c : c + 1, :] = rows[at : at + 1, :]
        turned[0, b * LANES : (b + 1) * LANES, :] = square[...].T
    for k in range(9):
        taps[8 * k : 8 * k + 8, :] = turned[0, pl.ds(k, LANES, stride=9), :].T[0:8, :]
    leave[...] = taps[...].astype(BF16)
    lane = lax.broadcasted_iota(jnp.int32, (8, LANES), 1)
    place = lax.broadcasted_iota(jnp.int32, (8, LANES), 0)
    chosen = jnp.logical_and(lane == place, place < 3)
    last = jnp.broadcast_to(rows[ROW.bias_out : ROW.bias_out + 1, :], (8, LANES))
    bias_out[...] = jnp.broadcast_to(
        jnp.sum(jnp.where(chosen, last, 0.0), axis=1, keepdims=True), (8, LANES)
    )


def prep_weights(flat, with_back):
    rows = flat.reshape(-1, LANES)
    shapes = dict(PREP_SHAPES)
    if with_back:
        shapes.update(BACK_SHAPES)
    whole = pl.BlockSpec(memory_space=pltpu.VMEM)
    made = pl.pallas_call(
        lambda *refs: prep_kernel(with_back, *refs),
        out_shape=[jax.ShapeDtypeStruct(s, BF16) for s in shapes.values()]
        + [
            jax.ShapeDtypeStruct((72, BASE), BF16),
            jax.ShapeDtypeStruct((72, BASE), BF16),
            jax.ShapeDtypeStruct((8, LANES), F32),
            jax.ShapeDtypeStruct((16, WIDE), F32),
            jax.ShapeDtypeStruct((8, TEMB), F32),
        ],
        in_specs=[whole],
        out_specs=[whole] * (len(shapes) + 5),
        scratch_shapes=[
            pltpu.VMEM((WIDE // LANES, 9 * WIDE, LANES), F32),
            pltpu.VMEM((LANES, LANES), F32),
            pltpu.VMEM((72, LANES), F32),
        ],
        compiler_params=pltpu.CompilerParams(vmem_limit_bytes=VMEM_LIMIT),
    )(rows)
    found = SimpleNamespace(**dict(zip(shapes, made)))
    found.enter, found.leave, found.bias_out, found.vec, found.bias_hidden = made[-5:]
    return found


def forward_set(found):
    return dict(
        {name: getattr(found, name) for name in PREP_SHAPES},
        vec=found.vec,
        bias_hidden=found.bias_hidden,
        enter=found.enter,
        leave=found.leave,
        bias_out=found.bias_out,
    )


def back_set(found):
    return {name: getattr(found, name) for name in BACK_SHAPES}


def move_x(values, distance):
    if distance == 0:
        return values
    column = lax.broadcasted_iota(jnp.int32, values.shape, 0) % HALF
    keep = column < HALF - 1 if distance > 0 else column >= 1
    rolled = pltpu.roll(values, (-distance) % values.shape[0], axis=0)
    return jnp.where(keep, rolled, 0.0)


def move_plane(values, ys, xs):
    if ys == 0 and xs == 0:
        return values
    lane = lax.broadcasted_iota(jnp.int32, values.shape, 1)
    row, column = lane // HALF, lane % HALF
    keep = None
    for place, step in ((row, ys), (column, xs)):
        if step:
            test = place < HALF - 1 if step > 0 else place >= 1
            keep = test if keep is None else jnp.logical_and(keep, test)
    rolled = pltpu.roll(values, (-(HALF * ys + xs)) % PIX, axis=1)
    return jnp.where(keep, rolled, 0.0)


def source_of(phase, step):
    return (phase + step) % 2, (phase + step) // 2


def silu_and_slope(values):
    gate = 1.0 / (1.0 + jnp.exp(-values))
    return values * gate, gate * (1.0 + values * (1.0 - gate))


def silu(values):
    return values * (1.0 / (1.0 + jnp.exp(-values)))


def column_sum(values):
    return jnp.sum(values, axis=0, keepdims=True)


def group_sum(vectors, members):
    stacked = jnp.concatenate(vectors + [jnp.zeros((8 - len(vectors), WIDE), F32)], axis=0)
    high = stacked.astype(BF16).astype(F32)
    rest = stacked - high
    middle = rest.astype(BF16).astype(F32)
    parts = jnp.concatenate([high, middle, rest - middle, jnp.zeros_like(high)], axis=0)
    summed = dot(parts.astype(BF16), members[...])
    total = summed[0:8] + summed[8:16] + summed[16:24]
    return [total[i : i + 1] for i in range(len(vectors))]


def norm_stats(blocks, members, count):
    total = sum(column_sum(block) for block in blocks)
    (mean,) = group_sum([total], members)
    mean = mean * (1.0 / count)
    square = sum(column_sum((block - mean) * (block - mean)) for block in blocks)
    (spread,) = group_sum([square], members)
    return mean, lax.rsqrt(spread * (1.0 / count) + 1e-05)


def norm_back(grads, hats, gain, scale, members, count):
    plain = sum(column_sum(grad) for grad in grads)
    weighted = sum(column_sum(grad * hat) for grad, hat in zip(grads, hats))
    mean_plain, mean_weighted = group_sum([plain * gain, weighted * gain], members)
    mean_plain = mean_plain * (1.0 / count)
    mean_weighted = mean_weighted * (1.0 / count)
    inputs = [
        scale * (grad * gain - mean_plain - hat * mean_weighted) for grad, hat in zip(grads, hats)
    ]
    return inputs, weighted, plain


NORM_WIDE = PIX * (WIDE // GROUPS)
NORM_BASE = 4 * PIX * (BASE // GROUPS)


def network_kernel(images_here, param_rows, given, made, scratch, *refs):
    teach, learn, r = SimpleNamespace(), SimpleNamespace(), SimpleNamespace()
    owners = [r] * len(given[0]) + [teach] * len(given[1]) + [learn] * len(given[2])
    owners += [r] * (len(made) + len(scratch))
    names = list(given[0]) + list(given[1]) + list(given[2]) + list(made) + list(scratch)
    for owner, name, ref in zip(owners, names, refs, strict=True):
        setattr(owner, name, ref)
    taps, taps_turned, first = r.taps, r.taps_turned, r.first
    cat_down, cat, cat_up = r.cat_down, r.cat, r.cat_up
    wide, base = r.members_wide, r.members_base

    lane = lax.broadcasted_iota(jnp.int32, (WIDE, WIDE), 1)
    row = lax.broadcasted_iota(jnp.int32, (WIDE, WIDE), 0)
    per_wide, per_base = WIDE // GROUPS, BASE // GROUPS
    wide[...] = jnp.where(lane // per_wide == row // per_wide, 1.0, 0.0).astype(BF16)
    base[...] = jnp.where(
        (lane % BASE) // per_base == (row % BASE) // per_base, 1.0, 0.0
    ).astype(BF16)
    for ref in (r.cat_down, r.cat, r.cat_up):
        ref[...] = jnp.zeros_like(ref)
    for ref in (r.acc_down, r.acc_one, r.acc_two, r.acc_up, r.acc_inner, r.acc_outer, r.acc_vec):
        ref[...] = jnp.zeros_like(ref)
    for ref in (r.grad_in, r.grad_out, r.small, r.hidden_low, r.grad_shift):
        ref[...] = jnp.zeros_like(ref)

    def vector(who, place):
        return who.vec[place : place + 1, :]

    def add_vector(place, value):
        r.acc_vec[place : place + 1, :] += value

    def time_path(who, embed, shift_ref, keep):
        pre = dot(embed[...].astype(BF16), who.time_one[...]) + who.bias_hidden[...]
        hidden = silu(pre)
        shift_ref[...] = dot(hidden.astype(BF16), who.time_two[...]) + vector(who, VEC.time_bias_two)
        if keep:
            r.hidden[...] = pre
            r.hidden_low[0:8, :] = hidden

    time_path(teach, r.embed_one, r.shift_t1, False)
    time_path(teach, r.embed_two, r.shift_t2, False)
    time_path(learn, r.embed_one, r.shift_s, True)

    def set_taps(plane, sign, taps):
        quarters = [plane[:, p * PIX : (p + 1) * PIX] for p in range(4)]
        for py in range(2):
            for px in range(2):
                p = 2 * py + px
                blocks = []
                for ky in range(3):
                    for kx in range(3):
                        sy, ys = source_of(py, sign * (ky - 1))
                        sx, xs = source_of(px, sign * (kx - 1))
                        blocks.append(move_plane(quarters[2 * sy + sx], ys, xs))
                column = jnp.concatenate(blocks, axis=0)
                taps[:, p * PIX : (p + 1) * PIX] = column.astype(BF16)
                taps_turned[p] = column.T.astype(BF16)

    def set_cat(values):
        for kx in range(3):
            cat[HALF : HALF + PIX, kx * WIDE : (kx + 1) * WIDE] = move_x(values, kx - 1).astype(
                BF16
            )

    def convolve(kernel):
        return sum(dot(cat[ky * HALF : ky * HALF + PIX, :], kernel[ky]) for ky in range(3))

    def forward(who, plane, shift, keep):
        set_taps(plane, 1, taps)
        bias = vector(who, VEC.bias_in)[:, 0:BASE]
        for py in range(2):
            for px in range(2):
                first[py, :, px * BASE : (px + 1) * BASE] = (
                    dot(taps_turned[2 * py + px], who.enter[...]) + bias
                )
        for py in range(2):
            even, odd = first[py, :, 0:BASE], first[py, :, BASE:]
            cat_down[py, HALF:, 0:BASE] = move_x(odd, -1).astype(BF16)
            cat_down[py, HALF:, BASE : 2 * BASE] = even.astype(BF16)
            cat_down[py, HALF:, 2 * BASE :] = odd.astype(BF16)
            if keep:
                r.first_turned[py] = first[py].T.astype(BF16)
        kernel = who.down
        down = (
            dot(cat_down[1, 0:PIX, :], kernel[0])
            + dot(cat_down[0, HALF:, :], kernel[1])
            + dot(cat_down[1, HALF:, :], kernel[2])
            + vector(who, VEC.bias_down)
        )
        r.down[...] = down
        stats_one = norm_stats([down], wide, NORM_WIDE)
        hat = (r.down[...] - stats_one[0]) * stats_one[1]
        branch = silu(
            hat * vector(who, VEC.norm_one_gain) + vector(who, VEC.norm_one_shift)
        )
        set_cat(branch)
        if keep:
            r.one_turned[...] = branch.T.astype(BF16)
        branch = convolve(who.one) + (vector(who, VEC.bias_one) + shift)
        r.branch[...] = branch
        stats_two = norm_stats([branch], wide, NORM_WIDE)
        hat = (r.branch[...] - stats_two[0]) * stats_two[1]
        branch = silu(
            hat * vector(who, VEC.norm_two_gain) + vector(who, VEC.norm_two_shift)
        )
        set_cat(branch)
        if keep:
            r.two_turned[...] = branch.T.astype(BF16)
        middle = r.down[...] + convolve(who.two) + vector(who, VEC.bias_two)
        r.middle[...] = middle
        stats_attn = norm_stats([middle], wide, NORM_WIDE)
        hat = (r.middle[...] - stats_attn[0]) * stats_attn[1]
        tokens = hat * vector(who, VEC.attn_gain) + vector(who, VEC.attn_shift)
        if keep:
            r.tokens_turned[...] = tokens.T.astype(BF16)
        joined = r.joined
        joined[...] = dot(tokens.astype(BF16), who.inner[...]).astype(BF16)
        scores = lax.dot_general(
            joined[:, 0:WIDE],
            joined[:, WIDE : 2 * WIDE],
            (((1,), (1,)), ((), ())),
            preferred_element_type=F32,
        ) * (WIDE**-0.5)
        weights = jnp.exp(scores - jnp.max(scores, axis=1, keepdims=True))
        weights = weights / jnp.sum(weights, axis=1, keepdims=True)
        if keep:
            r.soft[...] = weights
        mixed = dot(weights.astype(BF16), joined[:, 2 * WIDE :])
        if keep:
            r.mixed[...] = mixed
        result = dot(mixed.astype(BF16), who.outer[...]) + vector(who, VEC.attn_bias)
        middle_two = r.middle[...] + result
        set_cat(middle_two)
        if keep:
            r.middle_turned[...] = middle_two.T.astype(BF16)
        upper = r.upper
        kernel = who.up
        for py in range(2):
            upper[py] = (
                dot(cat[py * HALF : py * HALF + PIX, :], kernel[2 * py])
                + dot(cat[(py + 1) * HALF : (py + 1) * HALF + PIX, :], kernel[2 * py + 1])
                + vector(who, VEC.bias_up)
                + first[py]
            )
        stats_out = norm_stats([upper[0], upper[1]], base, NORM_BASE)
        replies = []
        for py in range(2):
            hat = (upper[py] - stats_out[0]) * stats_out[1]
            ending = silu(
                hat * vector(who, VEC.norm_out_gain) + vector(who, VEC.norm_out_shift)
            ).astype(BF16)
            if keep:
                r.end[py] = ending
            for px in range(2):
                replies.append(
                    lax.dot_general(
                        who.leave[...],
                        ending[:, px * BASE : (px + 1) * BASE],
                        (((1,), (1,)), ((), ())),
                        preferred_element_type=F32,
                    )
                )
        outs = []
        for py in range(2):
            for px in range(2):
                total = None
                for ky in range(3):
                    for kx in range(3):
                        sy, ys = source_of(py, ky - 1)
                        sx, xs = source_of(px, kx - 1)
                        k = 3 * ky + kx
                        term = move_plane(replies[2 * sy + sx][8 * k : 8 * k + 8, :], ys, xs)
                        total = term if total is None else total + term
                outs.append(total)
        guess = jnp.concatenate(outs, axis=1) + who.bias_out[:, 0:1]
        return guess, stats_one, stats_two, stats_attn, stats_out

    def image_step(index, carry):
        at = pl.ds(index, 1)
        plane = r.planes[index]
        coef = [r.coef[index, j] for j in range(5)]
        guess_one = forward(teach, plane, r.shift_t1[at, :], False)[0]
        middle_state = coef[0] * guess_one + coef[1] * plane
        guess_two = forward(teach, middle_state, r.shift_t2[at, :], False)[0]
        target = coef[2] * guess_one + coef[3] * guess_two
        guess, stats_one, stats_two, stats_attn, stats_out = forward(
            learn, plane, r.shift_s[at, :], True
        )
        error = guess - target
        weight = coef[4] * (1.0 / (3 * 4 * PIX))
        loss = jnp.sum(jnp.sum(error * error, axis=1, keepdims=True), axis=0, keepdims=True)
        r.small[8:9, :] += jnp.broadcast_to(loss * weight, (1, LANES))
        grad_guess = (2.0 * weight) * error
        r.small[0:8, :] += jnp.broadcast_to(
            jnp.sum(grad_guess, axis=1, keepdims=True), (8, LANES)
        )
        set_taps(grad_guess, -1, r.taps_back)
        total_out = None
        ends = r.end
        grads = []
        for py in range(2):
            parts = []
            for px in range(2):
                p = 2 * py + px
                term = dot(
                    r.taps_back[:, p * PIX : (p + 1) * PIX], ends[py, :, px * BASE : (px + 1) * BASE]
                )
                total_out = term if total_out is None else total_out + term
                parts.append(dot(taps_turned[p], learn.leave[...]))
            grads.append(jnp.concatenate(parts, axis=1))
        r.grad_out[...] += total_out
        gain = vector(learn, VEC.norm_out_gain)
        upper = r.upper
        hats = [(upper[py] - stats_out[0]) * stats_out[1] for py in range(2)]
        slopes = [
            silu_and_slope(hat * gain + vector(learn, VEC.norm_out_shift))[1] for hat in hats
        ]
        grads = [grad * slope for grad, slope in zip(grads, slopes)]
        grads, grad_gain, grad_bias = norm_back(grads, hats, gain, stats_out[1], base, NORM_BASE)
        add_vector(VEC.norm_out_gain, grad_gain)
        add_vector(VEC.norm_out_shift, grad_bias)
        add_vector(VEC.bias_up, column_sum(grads[0]) + column_sum(grads[1]))
        for py in range(2):
            upper[py] = grads[py]
            even, odd = grads[py][:, 0:BASE], grads[py][:, BASE:]
            middle_rows = slice(HALF, HALF + PIX)
            cat_up[py, middle_rows, 0:BASE] = move_x(even, 1).astype(BF16)
            cat_up[py, middle_rows, BASE : 2 * BASE] = even.astype(BF16)
            cat_up[py, middle_rows, 2 * BASE : 3 * BASE] = odd.astype(BF16)
            cat_up[py, middle_rows, 3 * BASE :] = move_x(odd, -1).astype(BF16)
        grad_middle = None
        for py in range(2):
            for ty in range(2):
                low = (2 - py - ty) * HALF
                block = cat_up[py, low : low + PIX, :]
                r.acc_up[2 * py + ty] += dot(r.middle_turned[...], block)
                term = dot(block, learn.up_t[2 * py + ty])
                grad_middle = term if grad_middle is None else grad_middle + term
        add_vector(VEC.attn_bias, column_sum(grad_middle))
        grad_low = grad_middle.astype(BF16)
        joined = r.joined
        mixed = r.mixed[...]
        r.acc_outer[...] += dot(mixed.T.astype(BF16), grad_low)
        grad_mixed = dot(grad_low, learn.outer_t[...]).astype(BF16)
        soft = r.soft[...]
        grad_soft = lax.dot_general(
            grad_mixed, joined[:, 2 * WIDE :], (((1,), (1,)), ((), ())), preferred_element_type=F32
        )
        grad_value = dot(soft.T.astype(BF16), grad_mixed)
        grad_scores = soft * (grad_soft - jnp.sum(soft * grad_soft, axis=1, keepdims=True))
        grad_query = dot(grad_scores.astype(BF16), joined[:, WIDE : 2 * WIDE]) * (WIDE**-0.5)
        grad_key = dot(grad_scores.T.astype(BF16), joined[:, 0:WIDE]) * (WIDE**-0.5)
        joined[:, 0:WIDE] = grad_query.astype(BF16)
        joined[:, WIDE : 2 * WIDE] = grad_key.astype(BF16)
        joined[:, 2 * WIDE :] = grad_value.astype(BF16)
        r.acc_inner[...] += dot(r.tokens_turned[...], joined[...])
        grad_tokens = dot(joined[...], learn.inner_t[...])
        hat = (r.middle[...] - stats_attn[0]) * stats_attn[1]
        (back,), grad_gain, grad_bias = norm_back(
            [grad_tokens], [hat], vector(learn, VEC.attn_gain), stats_attn[1], wide, NORM_WIDE
        )
        add_vector(VEC.attn_gain, grad_gain)
        add_vector(VEC.attn_shift, grad_bias)
        grad_middle = grad_middle + back
        r.middle[...] = grad_middle
        add_vector(VEC.bias_two, column_sum(grad_middle))

        def conv_back(grad, acc, input_turned, kernel):
            for kx in range(3):
                cat[HALF : HALF + PIX, kx * WIDE : (kx + 1) * WIDE] = move_x(grad, 1 - kx).astype(
                    BF16
                )
            total = None
            for ky in range(3):
                low = (2 - ky) * HALF
                block = cat[low : low + PIX, :]
                acc[ky] += dot(input_turned[...], block)
                term = dot(block, kernel[ky])
                total = term if total is None else total + term
            return total

        def silu_norm_back(grad, place, stats, values):
            gain = vector(learn, place)
            hat = (values - stats[0]) * stats[1]
            slope = silu_and_slope(hat * gain + vector(learn, place + 1))[1]
            (back,), grad_gain, grad_bias = norm_back(
                [grad * slope], [hat], gain, stats[1], wide, NORM_WIDE
            )
            add_vector(place, grad_gain)
            add_vector(place + 1, grad_bias)
            return back

        grad_branch = conv_back(grad_middle, r.acc_two, r.two_turned, learn.two_t)
        grad_branch = silu_norm_back(grad_branch, VEC.norm_two_gain, stats_two, r.branch[...])
        bias_grad = column_sum(grad_branch)
        add_vector(VEC.bias_one, bias_grad)
        add_vector(VEC.time_bias_two, bias_grad)
        r.grad_shift[at, :] = bias_grad
        grad_branch = conv_back(grad_branch, r.acc_one, r.one_turned, learn.one_t)
        grad_down = r.middle[...] + silu_norm_back(
            grad_branch, VEC.norm_one_gain, stats_one, r.down[...]
        )
        add_vector(VEC.bias_down, column_sum(grad_down))
        cat[0:PIX, 0:WIDE] = move_x(grad_down, 1).astype(BF16)
        cat[0:PIX, WIDE : 2 * WIDE] = grad_down.astype(BF16)
        cat[PIX : PIX + HALF, :] = jnp.zeros((HALF, 3 * WIDE), BF16)
        here, below = cat[0:PIX, 0 : 2 * WIDE], cat[HALF : HALF + PIX, 0 : 2 * WIDE]
        kernel = learn.down_t
        grads = [
            dot(here, kernel[1]) + upper[0],
            dot(below, kernel[0]) + dot(here, kernel[2]) + upper[1],
        ]
        turned_first = r.first_turned
        r.acc_down[0] += dot(turned_first[1], below)
        r.acc_down[1] += dot(turned_first[0], here)
        r.acc_down[2] += dot(turned_first[1], here)
        cat[0:HALF, :] = jnp.zeros((HALF, 3 * WIDE), BF16)
        add_vector(VEC.bias_in, column_sum(grads[0]) + column_sum(grads[1]))
        total_in = None
        for py in range(2):
            for px in range(2):
                p = 2 * py + px
                term = dot(
                    taps[:, p * PIX : (p + 1) * PIX],
                    grads[py][:, px * BASE : (px + 1) * BASE].astype(BF16),
                )
                total_in = term if total_in is None else total_in + term
        r.grad_in[...] += total_in
        return carry

    lax.fori_loop(0, images_here, image_step, 0)

    grad_shift = r.grad_shift[...].astype(BF16)
    grad_two = dot(r.hidden_low[...].T.astype(BF16), grad_shift)
    pre = r.hidden[...]
    grad_hidden = dot(grad_shift, learn.time_two_t[...])[0:8, :] * silu_and_slope(pre)[1]
    grad_bias_hidden = column_sum(grad_hidden)
    pad = jnp.zeros((FREQ - 8, TEMB), F32)
    embed = jnp.concatenate([r.embed_one[...], pad[:, 0:FREQ]], axis=0)
    grad_one = dot(
        embed.T.astype(BF16), jnp.concatenate([grad_hidden, pad], axis=0).astype(BF16)
    )

    flat, turned, square = r.flat, r.turned, r.square
    last = ROW.bias_out
    flat[last:, :] = jnp.zeros((flat.shape[0] - last, LANES), F32)
    square[...] = jnp.zeros_like(square)
    for k in range(9):
        for c in range(3):
            square[9 * c + k : 9 * c + k + 1, :] = r.grad_in[8 * k + c : 8 * k + c + 1, :]
    low, high, offset, upper_part = narrow_places()
    spread = roll_rows(square[...].T, offset, 1)
    flat[0:27, :] = (
        dot(low.astype(BF16), jnp.where(upper_part, spread, 0.0).astype(BF16))
        + dot(high.astype(BF16), jnp.where(upper_part, 0.0, spread).astype(BF16))
    )[0:27, :]
    square[...] = jnp.zeros_like(square)
    for k in range(9):
        square[0:8, :] = r.grad_out[8 * k : 8 * k + 8, :]
        turned[0, pl.ds(k, LANES, stride=9), :] = square[...].T
    for b in range(9):
        block = turned[0, b * LANES : (b + 1) * LANES, :].T
        for c in range(3):
            at = ROW.conv_out + 9 * c + b
            flat[at : at + 1, :] = block[c : c + 1, :]
    lane = lax.broadcasted_iota(jnp.int32, (8, LANES), 1)
    place = lax.broadcasted_iota(jnp.int32, (8, LANES), 0)
    flat[last : last + 1, :] = column_sum(jnp.where(lane == place, r.small[0:8, :], 0.0))
    loss = r.small[8:9, :]
    high = loss.astype(BF16).astype(F32)
    middle = (loss - high).astype(BF16).astype(F32)
    count = r.coef[0, 5]
    for index in range(1, images_here):
        count = count + r.coef[index, 5]
    lane = lane[0:1, :]
    row = jnp.where(lane == 0, high, jnp.where(lane == 1, middle, loss - high - middle))
    row = jnp.where(lane == 3, count, jnp.where(lane < 3, row, 0.0))
    flat[pl.ds(param_rows + LOSS_GAP + r.place[0], 1), :] = row

    def unturn(start, wide_out, wide_in):
        count = wide_in * 9 // LANES
        for b in range(count):
            parts = [
                turned[c, b * LANES : (b + 1) * LANES, :].T for c in range(wide_out // LANES)
            ]
            block = parts[0] if len(parts) == 1 else jnp.concatenate(parts, axis=0)
            flat[pl.ds(start + b, wide_out, stride=count), :] = block

    def put_tap(k, value, wide_in):
        for c in range(0, value.shape[1], LANES):
            turned[c // LANES, pl.ds(k, wide_in, stride=9), :] = value[:, c : c + LANES]

    for start, acc in ((ROW.conv_one, r.acc_one), (ROW.conv_two, r.acc_two)):
        for ky in range(3):
            for kx in range(3):
                put_tap(3 * ky + kx, acc[ky, :, kx * WIDE : (kx + 1) * WIDE], WIDE)
        unturn(start, WIDE, WIDE)
    acc = r.acc_down
    for ky in range(3):
        put_tap(3 * ky, acc[ky, BASE:, 0:WIDE], BASE)
        put_tap(3 * ky + 1, acc[ky, 0:BASE, WIDE:], BASE)
        put_tap(3 * ky + 2, acc[ky, BASE:, WIDE:], BASE)
    unturn(ROW.conv_down, WIDE, BASE)
    acc = r.acc_up
    for ky in range(3):
        for kx in range(3):
            total = None
            for (py, ty), set_y in JOINT.items():
                for (px, tx), set_x in JOINT.items():
                    if ky in set_y and kx in set_x:
                        at = (2 * px + tx) * BASE
                        term = acc[2 * py + ty, :, at : at + BASE]
                        total = term if total is None else total + term
            put_tap(3 * ky + kx, total, WIDE)
    unturn(ROW.conv_up, BASE, WIDE)
    for start, value in (
        (ROW.attn_inner, r.acc_inner),
        (ROW.attn_outer, r.acc_outer),
        (ROW.time_one, grad_one),
        (ROW.time_two, grad_two),
    ):
        count = value.shape[1] // LANES
        for b in range(count):
            flat[pl.ds(start + b, value.shape[0], stride=count), :] = value[
                :, b * LANES : (b + 1) * LANES
            ]
    for place, at, narrow in VECTORS:
        low = r.acc_vec[place : place + 1, 0:LANES]
        high = r.acc_vec[place : place + 1, LANES:]
        if narrow:
            flat[at : at + 1, :] = low + high
        else:
            flat[at : at + 1, :] = low
            flat[at + 1 : at + 2, :] = high
    for b in range(TEMB // LANES):
        at = ROW.time_bias_one + b
        flat[at : at + 1, :] = grad_bias_hidden[:, b * LANES : (b + 1) * LANES]

    def narrow(index, carry):
        block = pl.ds(pl.multiple_of(index * UNIT, UNIT), UNIT)
        r.grad[block, :] = flat[block, :].astype(BF16)
        return carry

    lax.fori_loop(0, flat.shape[0] // UNIT, narrow, 0)


def network(planes, embed_one, embed_two, coef, place, teacher, student, param_rows, row_count):
    images_here = planes.shape[0]
    whole = pl.BlockSpec(memory_space=pltpu.VMEM)
    tall = PIX + 2 * HALF
    given = (
        dict(planes=planes, embed_one=embed_one, embed_two=embed_two, coef=coef, place=place),
        forward_set(teacher),
        dict(forward_set(student), **back_set(student)),
    )
    made = dict(
        grad=((row_count, LANES), BF16),
    )
    scratch = dict(
        members_wide=((WIDE, WIDE), BF16),
        members_base=((WIDE, WIDE), BF16),
        taps=((72, 4 * PIX), BF16),
        taps_back=((72, 4 * PIX), BF16),
        taps_turned=((4, PIX, 72), BF16),
        first=((2, PIX, WIDE), F32),
        cat_down=((2, PIX + HALF, 3 * BASE), BF16),
        cat=((tall, 3 * WIDE), BF16),
        cat_up=((2, tall, 2 * WIDE), BF16),
        down=((PIX, WIDE), F32),
        branch=((PIX, WIDE), F32),
        middle=((PIX, WIDE), F32),
        soft=((PIX, PIX), F32),
        joined=((PIX, 3 * WIDE), BF16),
        mixed=((PIX, WIDE), F32),
        upper=((2, PIX, WIDE), F32),
        end=((2, PIX, WIDE), BF16),
        first_turned=((2, WIDE, PIX), BF16),
        one_turned=((WIDE, PIX), BF16),
        two_turned=((WIDE, PIX), BF16),
        middle_turned=((WIDE, PIX), BF16),
        tokens_turned=((WIDE, PIX), BF16),
        shift_t1=((8, WIDE), F32),
        shift_t2=((8, WIDE), F32),
        shift_s=((8, WIDE), F32),
        hidden=((8, TEMB), F32),
        hidden_low=((LANES, TEMB), F32),
        grad_shift=((LANES, WIDE), F32),
        acc_down=((3, WIDE, 2 * WIDE), F32),
        acc_one=((3, WIDE, 3 * WIDE), F32),
        acc_two=((3, WIDE, 3 * WIDE), F32),
        acc_up=((4, WIDE, 2 * WIDE), F32),
        acc_inner=((WIDE, 3 * WIDE), F32),
        acc_outer=((WIDE, WIDE), F32),
        acc_vec=((16, WIDE), F32),
        turned=((WIDE // LANES, 9 * WIDE, LANES), F32),
        grad_in=((72, LANES), F32),
        grad_out=((72, LANES), F32),
        small=((16, LANES), F32),
        square=((LANES, LANES), F32),
        flat=((row_count, LANES), F32),
    )
    arrays = [array for group in given for array in group.values()]
    specs = [whole] * len(arrays)
    specs[3] = specs[4] = pl.BlockSpec(memory_space=pltpu.SMEM)
    return pl.pallas_call(
        lambda *refs: network_kernel(images_here, param_rows, given, made, scratch, *refs),
        out_shape=[jax.ShapeDtypeStruct(shape, kind) for shape, kind in made.values()],
        in_specs=specs,
        out_specs=[whole] * len(made),
        scratch_shapes=[pltpu.VMEM(shape, kind) for shape, kind in scratch.values()],
        compiler_params=pltpu.CompilerParams(vmem_limit_bytes=VMEM_LIMIT),
    )(*arrays)[0]


def chunk_rows(row_count, width):
    return -(-row_count // (width * UNIT)) * UNIT


def wave(times_now):
    half_freq = FREQ // 2
    freqs = jnp.exp(
        -math.log(10000.0) * jnp.arange(half_freq).astype(jnp.float32) / (half_freq - 1)
    )
    angles = 1000.0 * times_now[:, None] * freqs[None, :]
    return jnp.concatenate([jnp.sin(angles), jnp.cos(angles)], axis=1)


def local_gradient(images, noise, timesteps, counts, teacher, params, place, width):
    turns, slots = images.shape[0], images.shape[1]
    images_here = turns * slots
    times = (timesteps.astype(F32) / STEPS).reshape(images_here)
    times_mid = times - 0.5 / STEPS
    times_end = times - 1.0 / STEPS
    angle = 0.5 * math.pi
    alpha_now, sigma_now = jnp.cos(angle * times), jnp.sin(angle * times)
    sigma_mid, sigma_end = jnp.sin(angle * times_mid), jnp.sin(angle * times_end)
    step = math.pi / (4 * STEPS)
    slot_index = jnp.arange(slots, dtype=jnp.int32)
    valid = (slot_index[None, :] < counts[0][:, None]).astype(F32)
    weighting = valid.reshape(images_here) * (1.0 + (alpha_now / sigma_now) ** 2)
    coef = jnp.stack(
        [
            math.sin(step) / sigma_now,
            sigma_mid / sigma_now,
            sigma_end / (2.0 * math.cos(step) * sigma_mid),
            sigma_now / (2.0 * math.cos(step) * sigma_mid),
            weighting,
            valid.reshape(images_here),
        ],
        axis=1,
    )
    side = images.shape[-1]
    shape = (images_here, 3, side, side)
    noisy = (
        alpha_now[:, None, None, None] * images.reshape(shape)
        + sigma_now[:, None, None, None] * noise.reshape(shape)
    ).astype(BF16)
    planes = noisy.reshape(images_here, 3, HALF, 2, HALF, 2).transpose(0, 1, 3, 5, 2, 4)
    planes = jnp.pad(planes.reshape(images_here, 3, 4 * PIX), ((0, 0), (0, 5), (0, 0))).astype(F32)
    rows = ((0, 8 - images_here), (0, 0))
    embed_one, embed_two = jnp.pad(wave(times), rows), jnp.pad(wave(times_mid), rows)
    teacher_set = prep_weights(teacher.astype(F32), False)
    student_set = prep_weights(params, True)
    param_rows = params.shape[0] // LANES
    return network(
        planes,
        embed_one,
        embed_two,
        coef,
        place,
        teacher_set,
        student_set,
        param_rows,
        width * chunk_rows(param_rows, width),
    )


def remote(source, target, send, receive, place):
    return pltpu.make_async_remote_copy(
        src_ref=source,
        dst_ref=target,
        send_sem=send,
        recv_sem=receive,
        device_id=place,
        device_id_type=MESH,
    )


def greet(places):
    barrier = pltpu.get_barrier_semaphore()
    for place in places:
        pl.semaphore_signal(barrier, inc=1, device_id=place, device_id_type=MESH)
    pl.semaphore_wait(barrier, len(places))


def exchange_kernel(width, part, whole, near, partial, far, *sems):
    s_near, r_near, s_far, r_far, s_back, r_back, s_side, r_side = sems
    rows = part.shape[1] // PIECES
    half = width // 2
    grp, me = lax.axis_index("grp"), lax.axis_index("dp")
    side, along = lax.rem(me, 2), me // 2
    beside = (grp, me + 1 - 2 * side)
    others = []
    for step in range(1, half):
        other = lax.rem(along + step, half)
        others.append((other, (grp, 2 * other + side)))
    slot = side * half + along
    mine, yours = side * half, (1 - side) * half
    greet([beside] + [place for _, place in others])

    def span(piece):
        return pl.ds(piece * rows, rows)

    first = []
    for piece in range(PIECES):
        copy = remote(
            part.at[pl.ds(yours, half), span(piece)],
            near.at[:, span(piece)],
            s_near.at[piece],
            r_near.at[piece],
            beside,
        )
        copy.start()
        first.append(copy)
    second, third, fourth = [], [], []

    def hand_on(piece):
        first[piece].wait_recv()
        partial[:, span(piece)] = (
            part[pl.ds(mine, half), span(piece)].astype(F32) + near[:, span(piece)].astype(F32)
        ).astype(BF16)
        copies = []
        for index, (other, place) in enumerate(others):
            copy = remote(
                partial.at[other, span(piece)],
                far.at[index, span(piece)],
                s_far.at[piece, index],
                r_far.at[piece, index],
                place,
            )
            copy.start()
            copies.append(copy)
        second.append(copies)

    def finish(piece):
        total = part[slot, span(piece)].astype(F32) + near[along, span(piece)].astype(F32)
        for index, copy in enumerate(second[piece]):
            copy.wait_recv()
            total = total + far[index, span(piece)].astype(F32)
        whole[slot, span(piece)] = total.astype(BF16)
        copies = []
        for index, (_, place) in enumerate(others):
            copy = remote(
                whole.at[slot, span(piece)],
                whole.at[slot, span(piece)],
                s_back.at[piece, index],
                r_back.at[piece, index],
                place,
            )
            copy.start()
            copies.append(copy)
        third.append(copies)

    def pass_aside(piece):
        for copy in third[piece]:
            copy.wait_recv()
        copy = remote(
            whole.at[pl.ds(mine, half), span(piece)],
            whole.at[pl.ds(mine, half), span(piece)],
            s_side.at[piece],
            r_side.at[piece],
            beside,
        )
        copy.start()
        fourth.append(copy)

    for step in range(PIECES + 2):
        if step < PIECES:
            hand_on(step)
        if 1 <= step < PIECES + 1:
            finish(step - 1)
        if step >= 2:
            pass_aside(step - 2)
    for copy in fourth:
        copy.wait_recv()
    for copy in first + fourth:
        copy.wait_send()
    for copies in second + third:
        for copy in copies:
            copy.wait_send()


def exchange(part):
    width = lax.axis_size("dp")
    rows = part.shape[0] // width
    half = width // 2
    inside = pl.BlockSpec(memory_space=pltpu.VMEM)
    dma = pltpu.SemaphoreType.DMA
    whole = pl.pallas_call(
        lambda *refs: exchange_kernel(width, *refs),
        out_shape=jax.ShapeDtypeStruct((width, rows, LANES), BF16),
        in_specs=[inside],
        out_specs=inside,
        scratch_shapes=[
            pltpu.VMEM((half, rows, LANES), BF16),
            pltpu.VMEM((half, rows, LANES), BF16),
            pltpu.VMEM((half - 1, rows, LANES), BF16),
            dma((PIECES,)),
            dma((PIECES,)),
            dma((PIECES, half - 1)),
            dma((PIECES, half - 1)),
            dma((PIECES, half - 1)),
            dma((PIECES, half - 1)),
            dma((PIECES,)),
            dma((PIECES,)),
        ],
        compiler_params=pltpu.CompilerParams(
            collective_id=1, has_side_effects=True, vmem_limit_bytes=VMEM_LIMIT
        ),
    )(part.reshape(width, rows, LANES))
    return whole.reshape(width * rows, LANES)


def average_kernel(width, groups, diff, mean, near, *sems):
    s_near, r_near, s_far, r_far, s_side, r_side, s_cross, r_cross, s_core, r_core = sems
    part = diff.shape[1] // groups
    rows = part // PIECES
    half = width // 2
    grp, me = lax.axis_index("grp"), lax.axis_index("dp")
    side, along = lax.rem(me, 2), me // 2
    beside = (grp, me + 1 - 2 * side)
    core = lax.rem(grp, 2)
    plane = grp // 2
    crossed = lax.rem(grp + groups // 2, groups)
    across = (crossed, me)
    twin = (grp + 1 - 2 * core, me)
    others = []
    for step in range(1, half):
        other = lax.rem(along + step, half)
        others.append((other, (grp, 2 * other + side)))
    peers = []
    for step in range(1, groups):
        peer = lax.rem(grp + step, groups)
        peers.append((peer, (peer, me)))
    slot = side * half + along
    mine, yours = side * half, (1 - side) * half
    greet([beside] + [place for _, place in others] + [place for _, place in peers])

    def span(owner, piece):
        return pl.ds(owner * part + piece * rows, rows)

    sent = []

    def send(source, target, semaphore, other_semaphore, place):
        copy = remote(source, target, semaphore, other_semaphore, place)
        copy.start()
        sent.append(copy)
        return copy

    gathered, sided, crossed_one, crossed_two = [], [], [], []
    first = []
    for piece in range(PIECES):
        first.append(
            [
                send(
                    diff.at[slot, span(peer, piece)],
                    near.at[index, pl.ds(piece * rows, rows)],
                    s_near.at[piece, index],
                    r_near.at[piece, index],
                    place,
                )
                for index, (peer, place) in enumerate(peers)
            ]
        )

    def add_up(piece):
        total = diff[slot, span(grp, piece)].astype(F32)
        for index, copy in enumerate(first[piece]):
            copy.wait_recv()
            total = total + near[index, pl.ds(piece * rows, rows)].astype(F32)
        mean[slot, span(grp, piece)] = (total * (1.0 / groups)).astype(BF16)
        here = mean.at[slot, span(grp, piece)]
        gathered.append(
            [
                send(here, here, s_far.at[piece, index], r_far.at[piece, index], place)
                for index, (_, place) in enumerate(others)
            ]
        )

    def pass_aside(piece):
        for copy in gathered[piece]:
            copy.wait_recv()
        here = mean.at[pl.ds(mine, half), span(grp, piece)]
        sided.append(send(here, here, s_side.at[piece], r_side.at[piece], beside))
        crossed_one.append(send(here, here, s_cross.at[piece, 0], r_cross.at[piece, 0], across))

    def pass_across(piece):
        sided[piece].wait_recv()
        here = mean.at[pl.ds(yours, half), span(grp, piece)]
        crossed_two.append(send(here, here, s_cross.at[piece, 1], r_cross.at[piece, 1], across))
        here = mean.at[:, span(grp, piece)]
        last.append(send(here, here, s_core.at[piece, 0], r_core.at[piece, 0], twin))

    def pass_twin(piece):
        crossed_one[piece].wait_recv()
        crossed_two[piece].wait_recv()
        here = mean.at[:, span(crossed, piece)]
        last.append(send(here, here, s_core.at[piece, 1], r_core.at[piece, 1], twin))

    last = []
    for step in range(PIECES + 3):
        for lag, stage in enumerate((add_up, pass_aside, pass_across, pass_twin)):
            if 0 <= step - lag < PIECES:
                stage(step - lag)
    for copy in last:
        copy.wait_recv()
    for copy in sent:
        copy.wait_send()


def average_over_groups(diff):
    width, groups = lax.axis_size("dp"), lax.axis_size("grp")
    rows = diff.shape[0] // width
    half = width // 2
    inside = pl.BlockSpec(memory_space=pltpu.VMEM)
    dma = pltpu.SemaphoreType.DMA
    mean = pl.pallas_call(
        lambda *refs: average_kernel(width, groups, *refs),
        out_shape=jax.ShapeDtypeStruct((width, rows, LANES), BF16),
        in_specs=[inside],
        out_specs=inside,
        scratch_shapes=[
            pltpu.VMEM((groups - 1, rows // groups, LANES), BF16),
            dma((PIECES, groups - 1)),
            dma((PIECES, groups - 1)),
            dma((PIECES, half - 1)),
            dma((PIECES, half - 1)),
            dma((PIECES,)),
            dma((PIECES,)),
            dma((PIECES, 2)),
            dma((PIECES, 2)),
            dma((PIECES, 2)),
            dma((PIECES, 2)),
        ],
        compiler_params=pltpu.CompilerParams(
            collective_id=2, has_side_effects=True, vmem_limit_bytes=VMEM_LIMIT
        ),
    )(diff.reshape(width, rows, LANES))
    return mean.reshape(width * rows, LANES)


def adamw_update(gradient_sum, valid_total, square_total, start, first, second):
    norm_value = jnp.sqrt(square_total) / valid_total
    factor = CLIP_NORM / jnp.maximum(norm_value, CLIP_NORM) / valid_total
    clipped = gradient_sum * factor
    new_first = BETA_ONE * first + (1.0 - BETA_ONE) * clipped
    new_second = BETA_TWO * second + (1.0 - BETA_TWO) * clipped * clipped
    corrected = (
        new_first
        / (1.0 - BETA_ONE**STEP_COUNT)
        / (jnp.sqrt(new_second / (1.0 - BETA_TWO**STEP_COUNT)) + EPSILON)
    )
    return (RATE_INNER * (corrected + WEIGHT_DECAY * start), new_first, new_second, norm_value)


def outer_step(average, start, momentum):
    new_momentum = MOMENTUM_OUTER * momentum + average
    return (start - OUTER_RATE * (average + MOMENTUM_OUTER * new_momentum), new_momentum)


def local(
    images, noise, timesteps, counts, teacher, params, first_moment, second_moment, outer_momentum
):
    width = lax.axis_size("dp")
    place = lax.axis_index("dp").astype(jnp.int32)[None]
    part = local_gradient(images, noise, timesteps, counts, teacher, params, place, width)
    total = exchange(part)
    start = params.reshape(-1, LANES)
    count = start.shape[0]
    gradient = total[:count].astype(F32)
    begin = count + LOSS_GAP
    table = total[begin : begin + width, 0:4].astype(F32)
    loss_total, valid_total = jnp.sum(table[:, 0:3]), jnp.sum(table[:, 3])
    square_total = jnp.sum(gradient * gradient)
    diff, new_first, new_second, norm_value = adamw_update(
        gradient,
        valid_total,
        square_total,
        start,
        *lax.optimization_barrier(
            (first_moment.reshape(-1, LANES), second_moment.reshape(-1, LANES))
        ),
    )
    diff = jnp.pad(diff.astype(BF16), ((0, total.shape[0] - count), (0, 0)))
    average = average_over_groups(diff)[:count].astype(F32)
    new_weights, new_outer = outer_step(average, start, outer_momentum.reshape(-1, LANES))
    return (
        new_weights.reshape(-1),
        new_first.reshape(1, -1),
        new_second.reshape(1, -1),
        average.reshape(-1),
        new_outer.reshape(-1),
        loss_total[None],
        valid_total[None],
        norm_value[None],
    )


def solution(mesh):
    placed = (
        P(None, ("grp", "dp"), None, None, None),
        P(None, ("grp", "dp"), None, None, None),
        P(None, ("grp", "dp")),
        P(("grp", "dp"), None),
        P(),
        P(),
        P("grp", None),
        P("grp", None),
        P(),
    )
    return jax.shard_map(
        local,
        mesh=mesh,
        in_specs=placed,
        out_specs=(P(), P("grp", None), P("grp", None), P(), P(), P("grp"), P("grp"), P("grp")),
        check_vma=False,
    )
```

```python
import math
from types import SimpleNamespace

import jax
import jax.numpy as jnp
from jax import lax
from jax.experimental import pallas as pl
from jax.experimental.pallas import tpu as pltpu
from jax.sharding import PartitionSpec as P

BASE = 128
WIDE = 256
TEMB = 512
FREQ = 128
GROUPS = 32
STEPS = 64
STEP_COUNT = 10

BETA_ONE = 0.9
BETA_TWO = 0.999
EPSILON = 1e-08
RATE_INNER = 0.03
WEIGHT_DECAY = 0.01
CLIP_NORM = 0.005
OUTER_RATE = 0.7
MOMENTUM_OUTER = 0.9

F32 = jnp.float32
BF16 = jnp.bfloat16
LANES = 128
HALF = 16
PIX = HALF * HALF
VMEM_LIMIT = 60 * 1024 * 1024
MESH = pl.DeviceIdType.MESH
PIECES = 5
UNIT = 320


SIZES = dict(
    conv_in=BASE * 27,
    bias_in=BASE,
    conv_down=WIDE * BASE * 9,
    bias_down=WIDE,
    norm_one_gain=WIDE,
    norm_one_shift=WIDE,
    conv_one=WIDE * WIDE * 9,
    bias_one=WIDE,
    time_one=FREQ * TEMB,
    time_bias_one=TEMB,
    time_two=TEMB * WIDE,
    time_bias_two=WIDE,
    norm_two_gain=WIDE,
    norm_two_shift=WIDE,
    conv_two=WIDE * WIDE * 9,
    bias_two=WIDE,
    attn_gain=WIDE,
    attn_shift=WIDE,
    attn_inner=WIDE * 3 * WIDE,
    attn_outer=WIDE * WIDE,
    attn_bias=WIDE,
    conv_up=BASE * WIDE * 9,
    bias_up=BASE,
    norm_out_gain=BASE,
    norm_out_shift=BASE,
    conv_out=3 * BASE * 9,
    bias_out=3,
)


def layout():
    return list(SIZES.items())


def start_rows():
    found = {}
    offset = 0
    for name, number in layout():
        found[name] = offset // LANES
        offset += number
    return SimpleNamespace(**found)


ROW = start_rows()
VECTOR_PLACES = dict(
    bias_in=0,
    bias_down=1,
    norm_one_gain=2,
    norm_one_shift=3,
    bias_one=4,
    time_bias_two=5,
    norm_two_gain=6,
    norm_two_shift=7,
    bias_two=8,
    attn_gain=9,
    attn_shift=10,
    attn_bias=11,
    bias_up=12,
    norm_out_gain=13,
    norm_out_shift=14,
)
VEC = SimpleNamespace(**VECTOR_PLACES)
VECTORS = [(place, getattr(ROW, name), SIZES[name] == BASE) for name, place in VECTOR_PLACES.items()]
JOINT = {(0, 0): (0,), (0, 1): (1, 2), (1, 0): (0, 1), (1, 1): (2,)}

PREP_SHAPES = dict(
    down=(3, 3 * BASE, WIDE),
    one=(3, 3 * WIDE, WIDE),
    two=(3, 3 * WIDE, WIDE),
    inner=(WIDE, 3 * WIDE),
    outer=(WIDE, WIDE),
    up=(4, 3 * WIDE, WIDE),
    time_one=(FREQ, TEMB),
    time_two=(TEMB, WIDE),
)
BACK_SHAPES = dict(
    down_t=(3, 2 * WIDE, WIDE),
    one_t=(3, 3 * WIDE, WIDE),
    two_t=(3, 3 * WIDE, WIDE),
    up_t=(4, 2 * WIDE, WIDE),
)


NN = (((1,), (0,)), ((), ()))
NT = (((1,), (1,)), ((), ()))
TN = (((0,), (0,)), ((), ()))


def product(left, right, kind):
    return lax.dot_general(left, right, kind, preferred_element_type=F32)


def dot(left, right):
    return product(left, right, NN)


def narrow_places():
    begin = 27 * lax.broadcasted_iota(jnp.int32, (32, LANES), 1)
    row = lax.broadcasted_iota(jnp.int32, (32, LANES), 0)
    low = jnp.where(begin // LANES == row, 1.0, 0.0)
    high = jnp.where(begin // LANES + 1 == row, 1.0, 0.0)
    offset = (27 * lax.broadcasted_iota(jnp.int32, (LANES, LANES), 0)) % LANES
    lane = lax.broadcasted_iota(jnp.int32, (LANES, LANES), 1)
    return low, high, offset, lane >= offset


def roll_rows(values, offset, sign):
    for bit in range(7):
        moved = pltpu.roll(values, (sign << bit) % LANES, axis=1)
        values = jnp.where((offset >> bit) % 2 == 1, moved, values)
    return values


def prep_kernel(with_back, rows, *refs):
    if rows.dtype == BF16:
        rows, low, refs = refs[-1], rows, refs[:-1]
        step = low.shape[0] // 256 * 16

        def widen(index, carry):
            block = pl.ds(pl.multiple_of(index * step, 16), step)
            rows[block, :] = low[block, :].astype(F32)
            return carry

        lax.fori_loop(0, 16, widen, 0)
        rows[16 * step :, :] = low[16 * step :, :].astype(F32)
    names = list(PREP_SHAPES) + (list(BACK_SHAPES) if with_back else [])
    out = SimpleNamespace(**dict(zip(names, refs)))
    enter, leave, bias_out, vec, bias_hidden, turned, square, taps = refs[len(names) :]

    def turn(start, wide_out, wide_in):
        count = wide_in * 9 // LANES
        for b in range(count):
            block = rows[pl.ds(start + b, wide_out, stride=count), :].T
            for c in range(0, wide_out, LANES):
                turned[c // LANES, b * LANES : (b + 1) * LANES, :] = block[:, c : c + LANES]

    def tap(k, wide_out, wide_in):
        parts = [turned[c, pl.ds(k, wide_in, stride=9), :] for c in range(wide_out // LANES)]
        return parts[0] if len(parts) == 1 else jnp.concatenate(parts, axis=1)

    for start, place, place_t in (
        (ROW.conv_one, out.one, out.one_t if with_back else None),
        (ROW.conv_two, out.two, out.two_t if with_back else None),
    ):
        turn(start, WIDE, WIDE)
        for ky in range(3):
            for kx in range(3):
                block = tap(3 * ky + kx, WIDE, WIDE)
                place[ky, kx * WIDE : (kx + 1) * WIDE, :] = block.astype(BF16)
                if with_back:
                    place_t[ky, kx * WIDE : (kx + 1) * WIDE, :] = block.T.astype(BF16)
    turn(ROW.conv_down, WIDE, BASE)
    for ky in range(3):
        for kx in range(3):
            block = tap(3 * ky + kx, WIDE, BASE)
            out.down[ky, kx * BASE : (kx + 1) * BASE, :] = block.astype(BF16)
            if with_back:
                back = block.T.astype(BF16)
                if kx == 0:
                    out.down_t[ky, 0:WIDE, BASE:] = back
                elif kx == 1:
                    out.down_t[ky, 0:WIDE, 0:BASE] = jnp.zeros((WIDE, BASE), BF16)
                    out.down_t[ky, WIDE:, 0:BASE] = back
                else:
                    out.down_t[ky, WIDE:, BASE:] = back
    turn(ROW.conv_up, BASE, WIDE)
    for py in range(2):
        for ty in range(2):
            index = 2 * py + ty
            for px in range(2):
                for tx in range(2):
                    total = None
                    for ky in JOINT[py, ty]:
                        for kx in JOINT[px, tx]:
                            term = tap(3 * ky + kx, BASE, WIDE).astype(BF16).astype(F32)
                            total = term if total is None else total + term
                    xo = px + tx
                    out.up[index, xo * WIDE : (xo + 1) * WIDE, px * BASE : (px + 1) * BASE] = (
                        total.astype(BF16)
                    )
                    if with_back:
                        at = (2 * px + tx) * BASE
                        out.up_t[index, at : at + BASE, :] = total.T.astype(BF16)
                at = 2 * WIDE if px == 0 else 0
                out.up[index, at : at + WIDE, px * BASE : (px + 1) * BASE] = jnp.zeros(
                    (WIDE, BASE), BF16
                )
    for start, place in (
        (ROW.attn_inner, out.inner),
        (ROW.attn_outer, out.outer),
        (ROW.time_one, out.time_one),
        (ROW.time_two, out.time_two),
    ):
        height, width = place.shape
        count = width // LANES
        for b in range(count):
            block = rows[pl.ds(start + b, height, stride=count), :]
            place[:, b * LANES : (b + 1) * LANES] = block.astype(BF16)
    vec[...] = jnp.zeros_like(vec)
    for place, r, narrow in VECTORS:
        second = r if narrow else r + 1
        vec[place : place + 1, 0:LANES] = rows[r : r + 1, :]
        vec[place : place + 1, LANES:] = rows[second : second + 1, :]
    for b in range(TEMB // LANES):
        r = ROW.time_bias_one + b
        bias_hidden[:, b * LANES : (b + 1) * LANES] = jnp.broadcast_to(rows[r : r + 1, :], (8, LANES))
    low, high, offset, upper_part = narrow_places()
    block = rows[0:32, :].astype(BF16)
    merged = jnp.where(
        upper_part, dot(low.T.astype(BF16), block), dot(high.T.astype(BF16), block)
    )
    merged = roll_rows(merged, offset, -1).T
    taps[...] = jnp.zeros_like(taps)
    for k in range(9):
        for c in range(3):
            taps[8 * k + c : 8 * k + c + 1, :] = merged[9 * c + k : 9 * c + k + 1, :]
    enter[...] = taps[...].astype(BF16)
    square[...] = jnp.zeros_like(square)
    for b in range(9):
        for c in range(3):
            at = ROW.conv_out + 9 * c + b
            square[c : c + 1, :] = rows[at : at + 1, :]
        turned[0, b * LANES : (b + 1) * LANES, :] = square[...].T
    for k in range(9):
        taps[8 * k : 8 * k + 8, :] = turned[0, pl.ds(k, LANES, stride=9), :].T[0:8, :]
    leave[...] = taps[...].astype(BF16)
    lane = lax.broadcasted_iota(jnp.int32, (8, LANES), 1)
    place = lax.broadcasted_iota(jnp.int32, (8, LANES), 0)
    chosen = jnp.logical_and(lane == place, place < 3)
    last = jnp.broadcast_to(rows[ROW.bias_out : ROW.bias_out + 1, :], (8, LANES))
    bias_out[...] = jnp.broadcast_to(
        jnp.sum(jnp.where(chosen, last, 0.0), axis=1, keepdims=True), (8, LANES)
    )


def prep_weights(flat, with_back):
    rows = flat.reshape(-1, LANES)
    shapes = dict(PREP_SHAPES)
    if with_back:
        shapes.update(BACK_SHAPES)
    whole = pl.BlockSpec(memory_space=pltpu.VMEM)
    made = pl.pallas_call(
        lambda *refs: prep_kernel(with_back, *refs),
        out_shape=[jax.ShapeDtypeStruct(s, BF16) for s in shapes.values()]
        + [
            jax.ShapeDtypeStruct((72, BASE), BF16),
            jax.ShapeDtypeStruct((72, BASE), BF16),
            jax.ShapeDtypeStruct((8, LANES), F32),
            jax.ShapeDtypeStruct((16, WIDE), F32),
            jax.ShapeDtypeStruct((8, TEMB), F32),
        ],
        in_specs=[whole],
        out_specs=[whole] * (len(shapes) + 5),
        scratch_shapes=[
            pltpu.VMEM((WIDE // LANES, 9 * WIDE, LANES), F32),
            pltpu.VMEM((LANES, LANES), F32),
            pltpu.VMEM((72, LANES), F32),
        ]
        + ([pltpu.VMEM(rows.shape, F32)] if rows.dtype == BF16 else []),
        compiler_params=pltpu.CompilerParams(vmem_limit_bytes=VMEM_LIMIT),
    )(rows)
    found = SimpleNamespace(**dict(zip(shapes, made)))
    found.enter, found.leave, found.bias_out, found.vec, found.bias_hidden = made[-5:]
    return found


def forward_set(found):
    return dict(
        {name: getattr(found, name) for name in PREP_SHAPES},
        vec=found.vec,
        bias_hidden=found.bias_hidden,
        enter=found.enter,
        leave=found.leave,
        bias_out=found.bias_out,
    )


def back_set(found):
    return {name: getattr(found, name) for name in BACK_SHAPES}


def move_x(values, distance):
    if distance == 0:
        return values
    column = lax.broadcasted_iota(jnp.int32, values.shape, 0) % HALF
    keep = column < HALF - 1 if distance > 0 else column >= 1
    rolled = pltpu.roll(values, (-distance) % values.shape[0], axis=0)
    return jnp.where(keep, rolled, 0.0)


def move_plane(values, ys, xs):
    if ys == 0 and xs == 0:
        return values
    lane = lax.broadcasted_iota(jnp.int32, values.shape, 1)
    row, column = lane // HALF, lane % HALF
    keep = None
    for place, step in ((row, ys), (column, xs)):
        if step:
            test = place < HALF - 1 if step > 0 else place >= 1
            keep = test if keep is None else jnp.logical_and(keep, test)
    rolled = pltpu.roll(values, (-(HALF * ys + xs)) % PIX, axis=1)
    return jnp.where(keep, rolled, 0.0)


def source_of(phase, step):
    return (phase + step) % 2, (phase + step) // 2


def silu_slope(values):
    gate = 1.0 / (1.0 + jnp.exp(-values))
    return gate * (1.0 + values * (1.0 - gate))


def silu(values):
    return values * (1.0 / (1.0 + jnp.exp(-values)))


def column_sum(values):
    return jnp.sum(values, axis=0, keepdims=True)


def group_sum(vectors, members):
    rest = 8 - len(vectors)
    stacked = jnp.concatenate(vectors + ([jnp.zeros((rest, WIDE), F32)] if rest else []), axis=0)
    high = stacked.astype(BF16).astype(F32)
    rest = stacked - high
    middle = rest.astype(BF16).astype(F32)
    parts = jnp.concatenate([high, middle, rest - middle, jnp.zeros_like(high)], axis=0)
    summed = dot(parts.astype(BF16), members[...])
    total = summed[0:8] + summed[8:16] + summed[16:24]
    return [total[i : i + 1] for i in range(len(vectors))]


NORM_WIDE = PIX * (WIDE // GROUPS)
NORM_BASE = 4 * PIX * (BASE // GROUPS)


def network_kernel(images_here, stream_count, given, made, scratch, own, *refs):
    teach, learn, r = SimpleNamespace(), SimpleNamespace(), SimpleNamespace()
    owners = [r] * len(given[0]) + [teach] * len(given[1]) + [learn] * len(given[2])
    owners += [r] * (len(made) + len(scratch))
    names = list(given[0]) + list(given[1]) + list(given[2]) + list(made) + list(scratch)
    streams = []
    for _ in range(stream_count):
        streams.append(SimpleNamespace())
        owners += [streams[-1]] * len(own)
        names += list(own)
    for owner, name, ref in zip(owners, names, refs, strict=True):
        setattr(owner, name, ref)
    wide, base = r.members_wide, r.members_base
    once = images_here == stream_count

    lane = lax.broadcasted_iota(jnp.int32, (WIDE, WIDE), 1)
    row = lax.broadcasted_iota(jnp.int32, (WIDE, WIDE), 0)
    per_wide, per_base = WIDE // GROUPS, BASE // GROUPS
    wide[...] = jnp.where(lane // per_wide == row // per_wide, 1.0, 0.0).astype(BF16)
    base[...] = jnp.where(
        (lane % BASE) // per_base == (row % BASE) // per_base, 1.0, 0.0
    ).astype(BF16)
    for q in streams:
        for ref in (q.cat_down, q.cat, q.cat_up):
            ref[...] = jnp.zeros_like(ref)
    for ref in (r.acc_vec, r.small, r.hidden_low, r.grad_shift):
        ref[...] = jnp.zeros_like(ref)
    totals = (r.acc_down, r.acc_one, r.acc_two, r.acc_up, r.acc_inner, r.acc_outer)
    if not once:
        for ref in totals + (r.grad_in, r.grad_out):
            ref[...] = jnp.zeros_like(ref)

    def vector(who, place):
        return who.vec[place : place + 1, :]

    def add_vector(place, value):
        r.acc_vec[place : place + 1, :] += value

    def time_path(who, embed, shift_ref, keep):
        pre = dot(embed[...].astype(BF16), who.time_one[...]) + who.bias_hidden[...]
        hidden = silu(pre)
        shift_ref[...] = dot(hidden.astype(BF16), who.time_two[...]) + vector(who, VEC.time_bias_two)
        if keep:
            r.hidden[...] = pre
            r.hidden_low[0:8, :] = hidden

    time_path(teach, r.embed_one, r.shift_t1, False)
    time_path(teach, r.embed_two, r.shift_t2, False)
    time_path(learn, r.embed_one, r.shift_s, True)

    def rows_product(pairs, kind=NN):
        return SimpleNamespace(answer=answer_rows, pairs=pairs, kind=kind)

    def answer_rows(asked):
        total = None
        for index, (_, right) in enumerate(asked[0].pairs):
            lefts = [ask.pairs[index][0] for ask in asked]
            left = jnp.concatenate(lefts, axis=1 if asked[0].kind is TN else 0)
            term = product(left, right[...], asked[0].kind)
            total = term if total is None else total + term
        return jnp.split(total, len(asked), axis=0)

    def lanes_product(left, right):
        return SimpleNamespace(answer=answer_lanes, left=left, right=right)

    def answer_lanes(asked):
        right = jnp.concatenate([ask.right for ask in asked], axis=0)
        return jnp.split(product(asked[0].left[...], right, NT), len(asked), axis=1)

    def add_product(target, place, left, right, kind=TN):
        return SimpleNamespace(
            answer=answer_total, target=target, place=place, left=left, right=right, kind=kind
        )

    def answer_total(asked):
        ask = asked[0]
        left = jnp.concatenate([a.left for a in asked], axis=0 if ask.kind is TN else 1)
        right = jnp.concatenate([a.right for a in asked], axis=0)
        total = product(left, right, ask.kind)
        if once:
            ask.target[ask.place] = total
        else:
            ask.target[ask.place] += total
        return [None] * len(asked)

    def group_sums(vectors, members):
        return SimpleNamespace(answer=answer_sums, vectors=vectors, members=members)

    def answer_sums(asked):
        count = len(asked[0].vectors)
        every = [vector_ for ask in asked for vector_ in ask.vectors]
        found = group_sum(every, asked[0].members)
        return [found[count * i : count * (i + 1)] for i in range(len(asked))]

    def norm_stats(blocks, members, count):
        total = sum(column_sum(block[...]) for block in blocks)
        (mean,) = yield group_sums([total], members)
        mean = mean * (1.0 / count)
        square = None
        for block in blocks:
            off = block[...] - mean
            term = column_sum(off * off)
            square = term if square is None else square + term
        (spread,) = yield group_sums([square], members)
        return mean, lax.rsqrt(spread * (1.0 / count) + 1e-05)

    def norm_back(grads, hats, gain, scale, members, count):
        plain = sum(column_sum(grad) for grad in grads)
        weighted = sum(column_sum(grad * hat) for grad, hat in zip(grads, hats))
        mean_plain, mean_weighted = yield group_sums([plain * gain, weighted * gain], members)
        mean_plain = mean_plain * (1.0 / count)
        mean_weighted = mean_weighted * (1.0 / count)
        inputs = [
            scale * (grad * gain - mean_plain - hat * mean_weighted)
            for grad, hat in zip(grads, hats)
        ]
        return inputs, weighted, plain

    def image_stream(q, index):
        taps, taps_back, first = q.taps, q.taps_back, q.first
        cat_down, cat, cat_up, joined, upper = q.cat_down, q.cat, q.cat_up, q.joined, q.upper
        body = slice(HALF, HALF + PIX)

        def set_taps(plane, sign, target):
            quarters = [plane[:, p * PIX : (p + 1) * PIX] for p in range(4)]
            for py in range(2):
                for px in range(2):
                    p = 2 * py + px
                    blocks = []
                    for ky in range(3):
                        for kx in range(3):
                            sy, ys = source_of(py, sign * (ky - 1))
                            sx, xs = source_of(px, sign * (kx - 1))
                            blocks.append(move_plane(quarters[2 * sy + sx], ys, xs))
                    target[:, p * PIX : (p + 1) * PIX] = jnp.concatenate(blocks, axis=0).astype(BF16)

        def set_cat(values):
            for kx in range(3):
                cat[body, kx * WIDE : (kx + 1) * WIDE] = move_x(values, kx - 1).astype(BF16)

        def convolve(kernel):
            return rows_product(
                [(cat[ky * HALF : ky * HALF + PIX, :], kernel.at[ky]) for ky in range(3)]
            )

        def make_plane():
            height = 3 * 2 * HALF
            rows = pl.ds(index * height, height) if isinstance(index, int) else pl.ds(
                pl.multiple_of(index * height, height), height
            )
            noisy = r.coef[index, 6] * r.images[rows, :] + r.coef[index, 7] * r.noise[rows, :]
            x = lax.broadcasted_iota(jnp.int32, (2 * HALF, 2 * PIX), 0)
            lane = lax.broadcasted_iota(jnp.int32, (2 * HALF, 2 * PIX), 1)
            spread = jnp.where(x == 2 * (lane % HALF) + lane // PIX, 1.0, 0.0).astype(BF16)
            values = dot(noisy.astype(BF16), spread)
            y = lax.broadcasted_iota(jnp.int32, values.shape, 0) % (2 * HALF)
            lane = lax.broadcasted_iota(jnp.int32, values.shape, 1) % PIX
            kept = jnp.where(lane // HALF == y // 2, values, 0.0)
            halves = []
            for py in range(2):
                part = jnp.where(y % 2 == py, kept, 0.0)
                lines = [
                    column_sum(part[c * 2 * HALF : (c + 1) * 2 * HALF, :]) for c in range(3)
                ]
                halves.append(jnp.concatenate(lines + [jnp.zeros((5, 2 * PIX), F32)], axis=0))
            return jnp.concatenate(halves, axis=1)

        def forward(who, plane, shift, keep):
            set_taps(plane, 1, taps)
            yield
            bias = vector(who, VEC.bias_in)[:, 0:BASE]
            for py in range(2):
                for px in range(2):
                    p = 2 * py + px
                    found = yield rows_product(
                        [(taps[:, p * PIX : (p + 1) * PIX], who.enter)], TN
                    )
                    first[py, :, px * BASE : (px + 1) * BASE] = found + bias
            for py in range(2):
                even, odd = first[py, :, 0:BASE], first[py, :, BASE:]
                cat_down[py, HALF:, 0:BASE] = move_x(odd, -1).astype(BF16)
                cat_down[py, HALF:, BASE : 2 * BASE] = even.astype(BF16)
                cat_down[py, HALF:, 2 * BASE :] = odd.astype(BF16)
            found = yield rows_product(
                [
                    (cat_down[1, 0:PIX, :], who.down.at[0]),
                    (cat_down[0, HALF:, :], who.down.at[1]),
                    (cat_down[1, HALF:, :], who.down.at[2]),
                ]
            )
            q.down[...] = found + vector(who, VEC.bias_down)
            stats_one = yield from norm_stats([q.down], wide, NORM_WIDE)
            hat = (q.down[...] - stats_one[0]) * stats_one[1]
            branch = silu(hat * vector(who, VEC.norm_one_gain) + vector(who, VEC.norm_one_shift))
            set_cat(branch)
            if keep:
                q.one_low[...] = branch.astype(BF16)
            found = yield convolve(who.one)
            q.branch[...] = found + (vector(who, VEC.bias_one) + shift)
            stats_two = yield from norm_stats([q.branch], wide, NORM_WIDE)
            hat = (q.branch[...] - stats_two[0]) * stats_two[1]
            branch = silu(hat * vector(who, VEC.norm_two_gain) + vector(who, VEC.norm_two_shift))
            set_cat(branch)
            if keep:
                q.two_low[...] = branch.astype(BF16)
            found = yield convolve(who.two)
            q.middle[...] = q.down[...] + found + vector(who, VEC.bias_two)
            stats_attn = yield from norm_stats([q.middle], wide, NORM_WIDE)
            hat = (q.middle[...] - stats_attn[0]) * stats_attn[1]
            tokens = hat * vector(who, VEC.attn_gain) + vector(who, VEC.attn_shift)
            tokens = tokens.astype(BF16)
            if keep:
                q.tokens[...] = tokens
            found = yield rows_product([(tokens, who.inner)])
            joined[...] = found.astype(BF16)
            scores = product(joined[:, 0:WIDE], joined[:, WIDE : 2 * WIDE], NT) * (WIDE**-0.5)
            yield
            weights = jnp.exp(scores - jnp.max(scores, axis=1, keepdims=True))
            weights = weights / jnp.sum(weights, axis=1, keepdims=True)
            if keep:
                q.soft[...] = weights
            yield
            mixed = dot(weights.astype(BF16), joined[:, 2 * WIDE :]).astype(BF16)
            if keep:
                q.mixed[...] = mixed
            found = yield rows_product([(mixed, who.outer)])
            set_cat(q.middle[...] + (found + vector(who, VEC.attn_bias)))
            for py in range(2):
                found = yield rows_product(
                    [
                        (cat[low * HALF : low * HALF + PIX, :], who.up.at[py + low])
                        for low in (py, py + 1)
                    ]
                )
                upper[py] = found + vector(who, VEC.bias_up) + first[py]
            stats_out = yield from norm_stats([upper.at[0], upper.at[1]], base, NORM_BASE)
            replies = []
            for py in range(2):
                hat = (upper[py] - stats_out[0]) * stats_out[1]
                ending = silu(
                    hat * vector(who, VEC.norm_out_gain) + vector(who, VEC.norm_out_shift)
                ).astype(BF16)
                if keep:
                    q.end[py] = ending
                for px in range(2):
                    reply = yield lanes_product(who.leave, ending[:, px * BASE : (px + 1) * BASE])
                    replies.append(reply)
            outs = []
            for py in range(2):
                for px in range(2):
                    total = None
                    for ky in range(3):
                        for kx in range(3):
                            sy, ys = source_of(py, ky - 1)
                            sx, xs = source_of(px, kx - 1)
                            k = 3 * ky + kx
                            term = move_plane(replies[2 * sy + sx][8 * k : 8 * k + 8, :], ys, xs)
                            total = term if total is None else total + term
                    outs.append(total)
            guess = jnp.concatenate(outs, axis=1) + who.bias_out[:, 0:1]
            return guess, stats_one, stats_two, stats_attn, stats_out

        def conv_back(grad, acc, value, kernel):
            for kx in range(3):
                cat[body, kx * WIDE : (kx + 1) * WIDE] = move_x(grad, 1 - kx).astype(BF16)

            def block(ky):
                low = (2 - ky) * HALF
                return cat[low : low + PIX, :]

            found = yield rows_product([(block(ky), kernel.at[ky]) for ky in range(3)])
            for ky in range(3):
                yield add_product(acc, ky, value[...], block(ky))
            return found

        def silu_norm_back(grad, place, stats, values):
            gain = vector(learn, place)
            hat = (values - stats[0]) * stats[1]
            slope = silu_slope(hat * gain + vector(learn, place + 1))
            (back,), grad_gain, grad_bias = yield from norm_back(
                [grad * slope], [hat], gain, stats[1], wide, NORM_WIDE
            )
            add_vector(place, grad_gain)
            add_vector(place + 1, grad_bias)
            return back

        at = pl.ds(index, 1)
        coef = [r.coef[index, j] for j in range(5)]
        plane = make_plane()
        guess_one = (yield from forward(teach, plane, r.shift_t1[at, :], False))[0]
        middle_state = coef[0] * guess_one + coef[1] * plane
        guess_two = (yield from forward(teach, middle_state, r.shift_t2[at, :], False))[0]
        target = coef[2] * guess_one + coef[3] * guess_two
        guess, stats_one, stats_two, stats_attn, stats_out = yield from forward(
            learn, plane, r.shift_s[at, :], True
        )
        error = guess - target
        weight = coef[4] * (1.0 / (3 * 4 * PIX))
        loss = jnp.sum(jnp.sum(error * error, axis=1, keepdims=True), axis=0, keepdims=True)
        r.small[8:9, :] += jnp.broadcast_to(loss * weight, (1, LANES))
        grad_guess = (2.0 * weight) * error
        r.small[0:8, :] += jnp.broadcast_to(
            jnp.sum(grad_guess, axis=1, keepdims=True), (8, LANES)
        )
        set_taps(grad_guess, -1, taps_back)
        yield
        grads = []
        for py in range(2):
            parts = []
            for px in range(2):
                p = 2 * py + px
                part = yield rows_product(
                    [(taps_back[:, p * PIX : (p + 1) * PIX], learn.leave)], TN
                )
                parts.append(part)
            grads.append(jnp.concatenate(parts, axis=1))
        ends = [q.end[p // 2, :, (p % 2) * BASE : (p % 2 + 1) * BASE] for p in range(4)]
        yield add_product(
            r.grad_out, slice(None), taps_back[...], jnp.concatenate(ends, axis=0), NN
        )
        gain = vector(learn, VEC.norm_out_gain)
        hats = [(upper[py] - stats_out[0]) * stats_out[1] for py in range(2)]
        shift = vector(learn, VEC.norm_out_shift)
        grads = [grad * silu_slope(hat * gain + shift) for grad, hat in zip(grads, hats)]
        grads, grad_gain, grad_bias = yield from norm_back(
            grads, hats, gain, stats_out[1], base, NORM_BASE
        )
        add_vector(VEC.norm_out_gain, grad_gain)
        add_vector(VEC.norm_out_shift, grad_bias)
        add_vector(VEC.bias_up, column_sum(grads[0]) + column_sum(grads[1]))
        for py in range(2):
            upper[py] = grads[py]
            even, odd = grads[py][:, 0:BASE], grads[py][:, BASE:]
            cat_up[py, body, 0:BASE] = move_x(even, 1).astype(BF16)
            cat_up[py, body, BASE : 2 * BASE] = even.astype(BF16)
            cat_up[py, body, 2 * BASE : 3 * BASE] = odd.astype(BF16)
            cat_up[py, body, 3 * BASE :] = move_x(odd, -1).astype(BF16)
        blocks = []
        for place in range(4):
            py, low = place // 2, (2 - place // 2 - place % 2) * HALF
            blocks.append(cat_up[py, low : low + PIX, :])
        grad_middle = yield rows_product(
            [(block, learn.up_t.at[place]) for place, block in enumerate(blocks)]
        )
        for place in range(4):
            py, low = place // 2, (2 - place // 2 - place % 2) * HALF
            yield add_product(
                r.acc_up, place, cat[body, WIDE : 2 * WIDE], cat_up[py, low : low + PIX, :]
            )
        add_vector(VEC.attn_bias, column_sum(grad_middle))
        grad_low = grad_middle.astype(BF16)
        grad_mixed = yield rows_product([(grad_low, learn.outer)], NT)
        grad_mixed = grad_mixed.astype(BF16)
        yield add_product(r.acc_outer, slice(None), q.mixed[...], grad_low)
        soft = q.soft[...]
        grad_soft = product(grad_mixed, joined[:, 2 * WIDE :], NT)
        grad_value = product(soft.astype(BF16), grad_mixed, TN)
        yield
        grad_scores = soft * (grad_soft - jnp.sum(soft * grad_soft, axis=1, keepdims=True))
        grad_scores = grad_scores.astype(BF16)
        yield
        grad_query = dot(grad_scores, joined[:, WIDE : 2 * WIDE]) * (WIDE**-0.5)
        grad_key = product(grad_scores, joined[:, 0:WIDE], TN) * (WIDE**-0.5)
        joined[:, 0:WIDE] = grad_query.astype(BF16)
        joined[:, WIDE : 2 * WIDE] = grad_key.astype(BF16)
        joined[:, 2 * WIDE :] = grad_value.astype(BF16)
        grad_tokens = yield rows_product([(joined[...], learn.inner)], NT)
        yield add_product(r.acc_inner, slice(None), q.tokens[...], joined[...])
        hat = (q.middle[...] - stats_attn[0]) * stats_attn[1]
        (back,), grad_gain, grad_bias = yield from norm_back(
            [grad_tokens], [hat], vector(learn, VEC.attn_gain), stats_attn[1], wide, NORM_WIDE
        )
        add_vector(VEC.attn_gain, grad_gain)
        add_vector(VEC.attn_shift, grad_bias)
        grad_middle = grad_middle + back
        q.middle[...] = grad_middle
        add_vector(VEC.bias_two, column_sum(grad_middle))
        grad_branch = yield from conv_back(grad_middle, r.acc_two, q.two_low, learn.two_t)
        grad_branch = yield from silu_norm_back(
            grad_branch, VEC.norm_two_gain, stats_two, q.branch[...]
        )
        bias_grad = column_sum(grad_branch)
        add_vector(VEC.bias_one, bias_grad)
        add_vector(VEC.time_bias_two, bias_grad)
        r.grad_shift[at, :] = bias_grad
        grad_branch = yield from conv_back(grad_branch, r.acc_one, q.one_low, learn.one_t)
        back = yield from silu_norm_back(grad_branch, VEC.norm_one_gain, stats_one, q.down[...])
        grad_down = q.middle[...] + back
        add_vector(VEC.bias_down, column_sum(grad_down))
        cat[0:PIX, 0:WIDE] = move_x(grad_down, 1).astype(BF16)
        cat[0:PIX, WIDE : 2 * WIDE] = grad_down.astype(BF16)
        cat[PIX : PIX + HALF, :] = jnp.zeros((HALF, 3 * WIDE), BF16)
        here, below = slice(0, PIX), slice(HALF, HALF + PIX)
        pair = slice(0, 2 * WIDE)
        even = yield rows_product([(cat[here, pair], learn.down_t.at[1])])
        odd = yield rows_product(
            [(cat[below, pair], learn.down_t.at[0]), (cat[here, pair], learn.down_t.at[2])]
        )
        grads = [even + upper[0], odd + upper[1]]
        for ky, py, rows in ((0, 1, below), (1, 0, here), (2, 1, here)):
            yield add_product(r.acc_down, ky, cat_down[py, HALF:, BASE:], cat[rows, pair])
        if not once:
            cat[0:HALF, :] = jnp.zeros((HALF, 3 * WIDE), BF16)
        add_vector(VEC.bias_in, column_sum(grads[0]) + column_sum(grads[1]))
        ends = [
            grads[p // 2][:, (p % 2) * BASE : (p % 2 + 1) * BASE].astype(BF16) for p in range(4)
        ]
        yield add_product(r.grad_in, slice(None), taps[...], jnp.concatenate(ends, axis=0), NN)

    def images_step(step, carry):
        running = [image_stream(q, step * stream_count + i) for i, q in enumerate(streams)]
        answers = [None] * stream_count
        while running:
            asked = []
            for stream, answer in zip(running, answers):
                try:
                    asked.append(stream.send(answer))
                except StopIteration:
                    pass
            if len(asked) < len(running):
                break
            if asked[0] is not None:
                answers = asked[0].answer(asked)
            else:
                answers = [None] * stream_count
        return carry

    if once:
        images_step(0, 0)
    else:
        lax.fori_loop(0, images_here // stream_count, images_step, 0)

    grad_shift = r.grad_shift[...].astype(BF16)
    grad_two = product(r.hidden_low[...].astype(BF16), grad_shift, TN)
    pre = r.hidden[...]
    grad_hidden = product(grad_shift, learn.time_two[...], NT)[0:8, :] * silu_slope(pre)
    grad_bias_hidden = column_sum(grad_hidden)
    pad = jnp.zeros((FREQ - 8, TEMB), F32)
    embed = jnp.concatenate([r.embed_one[...], pad[:, 0:FREQ]], axis=0)
    grad_one = product(
        embed.astype(BF16), jnp.concatenate([grad_hidden, pad], axis=0).astype(BF16), TN
    )

    flat, turned, square = r.flat, r.turned, r.square
    last = ROW.bias_out
    flat[last:, :] = jnp.zeros((flat.shape[0] - last, LANES), F32)
    square[...] = jnp.zeros_like(square)
    for k in range(9):
        for c in range(3):
            square[9 * c + k : 9 * c + k + 1, :] = r.grad_in[8 * k + c : 8 * k + c + 1, :]
    low, high, offset, upper_part = narrow_places()
    spread = roll_rows(square[...].T, offset, 1)
    flat[0:27, :] = (
        dot(low.astype(BF16), jnp.where(upper_part, spread, 0.0).astype(BF16))
        + dot(high.astype(BF16), jnp.where(upper_part, 0.0, spread).astype(BF16))
    )[0:27, :]
    square[...] = jnp.zeros_like(square)
    for k in range(9):
        square[0:8, :] = r.grad_out[8 * k : 8 * k + 8, :]
        turned[0, pl.ds(k, LANES, stride=9), :] = square[...].T
    for b in range(9):
        block = turned[0, b * LANES : (b + 1) * LANES, :].T
        for c in range(3):
            at = ROW.conv_out + 9 * c + b
            flat[at : at + 1, :] = block[c : c + 1, :]
    lane = lax.broadcasted_iota(jnp.int32, (8, LANES), 1)
    place = lax.broadcasted_iota(jnp.int32, (8, LANES), 0)
    flat[last : last + 1, :] = column_sum(jnp.where(lane == place, r.small[0:8, :], 0.0))
    count = r.coef[0, 5]
    for index in range(1, images_here):
        count = count + r.coef[index, 5]
    row = lax.broadcasted_iota(jnp.int32, (8, LANES), 0)
    loss = jnp.broadcast_to(r.small[8:9, :], (8, LANES))
    r.tile[...] = jnp.where(row == 0, loss, jnp.where(row == 1, count, 0.0))

    def unturn(start, wide_out, wide_in):
        count = wide_in * 9 // LANES
        for b in range(count):
            parts = [
                turned[c, b * LANES : (b + 1) * LANES, :].T for c in range(wide_out // LANES)
            ]
            block = parts[0] if len(parts) == 1 else jnp.concatenate(parts, axis=0)
            flat[pl.ds(start + b, wide_out, stride=count), :] = block

    def put_tap(k, value, wide_in):
        for c in range(0, value.shape[1], LANES):
            turned[c // LANES, pl.ds(k, wide_in, stride=9), :] = value[:, c : c + LANES]

    for start, acc in ((ROW.conv_one, r.acc_one), (ROW.conv_two, r.acc_two)):
        for ky in range(3):
            for kx in range(3):
                put_tap(3 * ky + kx, acc[ky, :, kx * WIDE : (kx + 1) * WIDE], WIDE)
        unturn(start, WIDE, WIDE)
    acc = r.acc_down
    for ky in range(3):
        put_tap(3 * ky, acc[ky, BASE:, 0:WIDE], BASE)
        put_tap(3 * ky + 1, acc[ky, 0:BASE, WIDE:], BASE)
        put_tap(3 * ky + 2, acc[ky, BASE:, WIDE:], BASE)
    unturn(ROW.conv_down, WIDE, BASE)
    acc = r.acc_up
    for ky in range(3):
        for kx in range(3):
            total = None
            for (py, ty), set_y in JOINT.items():
                for (px, tx), set_x in JOINT.items():
                    if ky in set_y and kx in set_x:
                        at = (2 * px + tx) * BASE
                        term = acc[2 * py + ty, :, at : at + BASE]
                        total = term if total is None else total + term
            put_tap(3 * ky + kx, total, WIDE)
    unturn(ROW.conv_up, BASE, WIDE)
    for start, value in (
        (ROW.attn_inner, r.acc_inner),
        (ROW.attn_outer, r.acc_outer),
        (ROW.time_one, grad_one),
        (ROW.time_two, grad_two),
    ):
        count = value.shape[1] // LANES
        for b in range(count):
            flat[pl.ds(start + b, value.shape[0], stride=count), :] = value[
                :, b * LANES : (b + 1) * LANES
            ]
    for place, at, narrow in VECTORS:
        low = r.acc_vec[place : place + 1, 0:LANES]
        high = r.acc_vec[place : place + 1, LANES:]
        if narrow:
            flat[at : at + 1, :] = low + high
        else:
            flat[at : at + 1, :] = low
            flat[at + 1 : at + 2, :] = high
    for b in range(TEMB // LANES):
        at = ROW.time_bias_one + b
        flat[at : at + 1, :] = grad_bias_hidden[:, b * LANES : (b + 1) * LANES]

    def narrow(index, carry):
        block = pl.ds(pl.multiple_of(index * UNIT, UNIT), UNIT)
        r.grad[block, :] = flat[block, :].astype(BF16)
        return carry

    lax.fori_loop(0, flat.shape[0] // UNIT, narrow, 0)


def network(images, noise, embed_one, embed_two, coef, teacher, student, row_count):
    images_here = coef.shape[0]
    whole = pl.BlockSpec(memory_space=pltpu.VMEM)
    tall = PIX + 2 * HALF
    given = (
        dict(coef=coef, images=images, noise=noise, embed_one=embed_one, embed_two=embed_two),
        forward_set(teacher),
        dict(forward_set(student), **back_set(student)),
    )
    made = dict(
        grad=((row_count, LANES), BF16),
        tile=((8, LANES), F32),
    )
    scratch = dict(
        members_wide=((WIDE, WIDE), BF16),
        members_base=((WIDE, WIDE), BF16),
        shift_t1=((8, WIDE), F32),
        shift_t2=((8, WIDE), F32),
        shift_s=((8, WIDE), F32),
        hidden=((8, TEMB), F32),
        hidden_low=((LANES, TEMB), F32),
        grad_shift=((LANES, WIDE), F32),
        acc_down=((3, WIDE, 2 * WIDE), F32),
        acc_one=((3, WIDE, 3 * WIDE), F32),
        acc_two=((3, WIDE, 3 * WIDE), F32),
        acc_up=((4, WIDE, 2 * WIDE), F32),
        acc_inner=((WIDE, 3 * WIDE), F32),
        acc_outer=((WIDE, WIDE), F32),
        acc_vec=((16, WIDE), F32),
        turned=((WIDE // LANES, 9 * WIDE, LANES), F32),
        grad_in=((72, LANES), F32),
        grad_out=((72, LANES), F32),
        small=((16, LANES), F32),
        square=((LANES, LANES), F32),
        flat=((row_count, LANES), F32),
    )
    own = dict(
        taps=((72, 4 * PIX), BF16),
        taps_back=((72, 4 * PIX), BF16),
        first=((2, PIX, WIDE), F32),
        cat_down=((2, PIX + HALF, 3 * BASE), BF16),
        cat=((tall, 3 * WIDE), BF16),
        cat_up=((2, tall, 2 * WIDE), BF16),
        down=((PIX, WIDE), F32),
        branch=((PIX, WIDE), F32),
        middle=((PIX, WIDE), F32),
        soft=((PIX, PIX), F32),
        joined=((PIX, 3 * WIDE), BF16),
        mixed=((PIX, WIDE), BF16),
        upper=((2, PIX, WIDE), F32),
        end=((2, PIX, WIDE), BF16),
        one_low=((PIX, WIDE), BF16),
        two_low=((PIX, WIDE), BF16),
        tokens=((PIX, WIDE), BF16),
    )
    stream_count = max(n for n in (4, 2, 1) if images_here % n == 0)
    arrays = [array for group in given for array in group.values()]
    specs = [whole] * len(arrays)
    specs[0] = pl.BlockSpec(memory_space=pltpu.SMEM)
    return pl.pallas_call(
        lambda *refs: network_kernel(
            images_here, stream_count, given, made, scratch, own, *refs
        ),
        out_shape=[jax.ShapeDtypeStruct(shape, kind) for shape, kind in made.values()],
        in_specs=specs,
        out_specs=[whole] * len(made),
        scratch_shapes=[
            pltpu.VMEM(shape, kind)
            for shape, kind in list(scratch.values()) + list(own.values()) * stream_count
        ],
        compiler_params=pltpu.CompilerParams(vmem_limit_bytes=VMEM_LIMIT),
    )(*arrays)


def chunk_rows(row_count, width):
    return -(-row_count // (width * UNIT)) * UNIT


def wave(times_now):
    half_freq = FREQ // 2
    freqs = jnp.exp(
        -math.log(10000.0) * jnp.arange(half_freq).astype(jnp.float32) / (half_freq - 1)
    )
    angles = 1000.0 * times_now[:, None] * freqs[None, :]
    return jnp.concatenate([jnp.sin(angles), jnp.cos(angles)], axis=1)


def local_gradient(images, noise, timesteps, counts, teacher, params, width):
    turns, slots = images.shape[0], images.shape[1]
    images_here = turns * slots
    times = (timesteps.astype(F32) / STEPS).reshape(images_here)
    times_mid = times - 0.5 / STEPS
    times_end = times - 1.0 / STEPS
    angle = 0.5 * math.pi
    alpha_now, sigma_now = jnp.cos(angle * times), jnp.sin(angle * times)
    sigma_mid, sigma_end = jnp.sin(angle * times_mid), jnp.sin(angle * times_end)
    step = math.pi / (4 * STEPS)
    slot_index = jnp.arange(slots, dtype=jnp.int32)
    valid = (slot_index[None, :] < counts[0][:, None]).astype(F32)
    weighting = valid.reshape(images_here) * (1.0 + (alpha_now / sigma_now) ** 2)
    coef = jnp.stack(
        [
            math.sin(step) / sigma_now,
            sigma_mid / sigma_now,
            sigma_end / (2.0 * math.cos(step) * sigma_mid),
            sigma_now / (2.0 * math.cos(step) * sigma_mid),
            weighting,
            valid.reshape(images_here),
            alpha_now,
            sigma_now,
        ],
        axis=1,
    )
    rows = ((0, 8 - images_here), (0, 0))
    embed_one, embed_two = jnp.pad(wave(times), rows), jnp.pad(wave(times_mid), rows)
    teacher_set = prep_weights(teacher, False)
    student_set = prep_weights(params, True)
    param_rows = params.shape[0] // LANES
    return network(
        images.reshape(-1, images.shape[-1]),
        noise.reshape(-1, noise.shape[-1]),
        embed_one,
        embed_two,
        coef,
        teacher_set,
        student_set,
        width * chunk_rows(param_rows, width),
    )


def remote(source, target, send, receive, place):
    return pltpu.make_async_remote_copy(
        src_ref=source,
        dst_ref=target,
        send_sem=send,
        recv_sem=receive,
        device_id=place,
        device_id_type=MESH,
    )


def greet(places):
    barrier = pltpu.get_barrier_semaphore()
    for place in places:
        pl.semaphore_signal(barrier, inc=1, device_id=place, device_id_type=MESH)
    pl.semaphore_wait(barrier, len(places))


def exchange_kernel(
    width, groups, param_rows, part, tile, params, first, second, whole, mean, total_tile, *rest
):
    near, partial, far, start, old_first, old_second, steps, quarter, tiles, sums = rest[0:10]
    held = rest[10:13]
    s_near, r_near, s_far, r_far, s_back, r_back, s_side, r_side = rest[13:21]
    s_tile, r_tile, s_sums, r_sums, s_step, r_step = rest[21:27]
    s_along, r_along, s_mean, r_mean, s_cross, r_cross, s_core, r_core = rest[27:35]
    chunk = part.shape[1]
    rows = chunk // PIECES
    share = chunk // groups
    share_rows = share // PIECES
    half = width // 2
    grp, me = lax.axis_index("grp"), lax.axis_index("dp")
    side, along = lax.rem(me, 2), me // 2
    beside = (grp, me + 1 - 2 * side)
    crossed = lax.rem(grp + groups // 2, groups)
    across = (crossed, me)
    twin = (grp + 1 - 2 * lax.rem(grp, 2), me)
    others = []
    for step in range(1, half):
        other = lax.rem(along + step, half)
        others.append((other, (grp, 2 * other + side)))
    peers = []
    for step in range(1, groups):
        peer = lax.rem(grp + step, groups)
        peers.append((peer, (peer, me)))
    slot = side * half + along
    mine, yours = side * half, (1 - side) * half
    greet([beside] + [place for _, place in others] + [place for _, place in peers])
    sent = []

    def send(source, target, semaphore, other_semaphore, place):
        copy = remote(source, target, semaphore, other_semaphore, place)
        copy.start()
        sent.append(copy)
        return copy

    def span(piece):
        return pl.ds(piece * rows, rows)

    first_leg = [
        send(
            part.at[pl.ds(yours, half), span(piece)],
            near.at[:, span(piece)],
            s_near.at[piece],
            r_near.at[piece],
            beside,
        )
        for piece in range(PIECES)
    ]

    full, tail = param_rows // chunk, param_rows % chunk
    pairs = ((params, start), (first, old_first), (second, old_second))

    def own_copies(count):
        at = pl.multiple_of(slot * chunk, 8)
        return [
            pltpu.make_async_copy(source.at[pl.ds(at, count)], target.at[0:count], held[i])
            for i, (source, target) in enumerate(pairs)
        ]

    for _, target in pairs:
        target[...] = jnp.zeros_like(target)

    @pl.when(slot < full)
    def _():
        copies = own_copies(chunk)
        for copy in copies:
            copy.start()
        for copy in copies:
            copy.wait()

    if tail:

        @pl.when(slot == full)
        def _():
            copies = own_copies(tail)
            for copy in copies:
                copy.start()
            for copy in copies:
                copy.wait()

    second_leg, third_leg, fourth_leg = [], [], []

    def hand_on(piece):
        first_leg[piece].wait_recv()
        partial[:, span(piece)] = (
            part[pl.ds(mine, half), span(piece)].astype(F32) + near[:, span(piece)].astype(F32)
        ).astype(BF16)
        second_leg.append(
            [
                send(
                    partial.at[other, span(piece)],
                    far.at[index, span(piece)],
                    s_far.at[piece, index],
                    r_far.at[piece, index],
                    place,
                )
                for index, (other, place) in enumerate(others)
            ]
        )

    def finish(piece):
        total = part[slot, span(piece)].astype(F32) + near[along, span(piece)].astype(F32)
        for index, copy in enumerate(second_leg[piece]):
            copy.wait_recv()
            total = total + far[index, span(piece)].astype(F32)
        low = total.astype(BF16)
        whole[slot, span(piece)] = low
        low = low.astype(F32)
        return jnp.sum((low * low).reshape(-1, 8, LANES), axis=0)

    def give_back(piece):
        here = whole.at[slot, span(piece)]
        third_leg.append(
            [
                send(here, here, s_back.at[piece, index], r_back.at[piece, index], place)
                for index, (_, place) in enumerate(others)
            ]
        )

    def pass_aside(piece):
        for copy in third_leg[piece]:
            copy.wait_recv()
        here = whole.at[pl.ds(mine, half), span(piece)]
        fourth_leg.append(send(here, here, s_side.at[piece], r_side.at[piece], beside))

    squares = None
    for step in range(PIECES + 1):
        if step < PIECES:
            hand_on(step)
        if step >= 1:
            square = finish(step - 1)
            squares = square if squares is None else squares + square

    tiles[0, 0:8, :] = squares
    tiles[0, 8:16, :] = tile[...]
    copy = send(tiles.at[0], tiles.at[1], s_tile, r_tile, beside)
    copy.wait_recv()
    sums[along] = tiles[0] + tiles[1]
    copies = [
        send(sums.at[along], sums.at[along], s_sums.at[index], r_sums.at[index], place)
        for index, (_, place) in enumerate(others)
    ]
    give_back(0)
    give_back(1)
    for copy in copies:
        copy.wait_recv()
    summed = sums[0]
    for index in range(1, half):
        summed = summed + sums[index]
    square_total = jnp.sum(jnp.sum(summed[0:8], axis=1, keepdims=True), axis=0, keepdims=True)
    valid_total = summed[9:10, 0:1]
    norm_value = jnp.sqrt(square_total) / valid_total
    factor = CLIP_NORM / jnp.maximum(norm_value, CLIP_NORM) / valid_total
    total_tile[0:8, :] = summed[8:16]
    total_tile[8:16, :] = jnp.broadcast_to(norm_value, (8, LANES))
    total_tile[16:24, :] = jnp.broadcast_to(factor, (8, LANES))

    def share_span(owner, piece):
        return pl.ds(owner * share + piece * share_rows, share_rows)

    for begin in range(0, chunk, share):
        block = slice(begin, begin + share)
        diff = adamw_update(
            whole[slot, block].astype(F32), factor, start[block], old_first[block], old_second[block]
        )[0]
        steps[block] = diff.astype(BF16)
    leaving, gathered, sided, crossed_one, crossed_two, last = [], [], [], [], [], []
    for piece in range(PIECES):
        leaving.append(
            [
                send(
                    steps.at[share_span(peer, piece)],
                    quarter.at[index, pl.ds(piece * share_rows, share_rows)],
                    s_step.at[piece, index],
                    r_step.at[piece, index],
                    place,
                )
                for index, (peer, place) in enumerate(peers)
            ]
        )

    def add_up(piece):
        total = steps[share_span(grp, piece)].astype(F32)
        for index, copy in enumerate(leaving[piece]):
            copy.wait_recv()
            total = total + quarter[index, pl.ds(piece * share_rows, share_rows)].astype(F32)
        mean[slot, share_span(grp, piece)] = (total * (1.0 / groups)).astype(BF16)
        here = mean.at[slot, share_span(grp, piece)]
        gathered.append(
            [
                send(here, here, s_along.at[piece, index], r_along.at[piece, index], place)
                for index, (_, place) in enumerate(others)
            ]
        )

    def pass_mean(piece):
        for copy in gathered[piece]:
            copy.wait_recv()
        here = mean.at[pl.ds(mine, half), share_span(grp, piece)]
        sided.append(send(here, here, s_mean.at[piece], r_mean.at[piece], beside))
        crossed_one.append(send(here, here, s_cross.at[piece, 0], r_cross.at[piece, 0], across))

    def pass_across(piece):
        sided[piece].wait_recv()
        here = mean.at[pl.ds(yours, half), share_span(grp, piece)]
        crossed_two.append(send(here, here, s_cross.at[piece, 1], r_cross.at[piece, 1], across))
        here = mean.at[:, share_span(grp, piece)]
        last.append(send(here, here, s_core.at[piece, 0], r_core.at[piece, 0], twin))

    def pass_twin(piece):
        crossed_one[piece].wait_recv()
        crossed_two[piece].wait_recv()
        here = mean.at[:, share_span(crossed, piece)]
        last.append(send(here, here, s_core.at[piece, 1], r_core.at[piece, 1], twin))

    stages = (
        (add_up, 0),
        (pass_mean, 1),
        (pass_across, 2),
        (pass_twin, 3),
    )
    for step in range(PIECES + 3):
        if step + 2 < PIECES:
            give_back(step + 2)
        if step < PIECES:
            pass_aside(step)
        for stage, lag in stages:
            if 0 <= step - lag < PIECES:
                stage(step - lag)
    for copy in fourth_leg + last:
        copy.wait_recv()
    for copy in sent:
        copy.wait_send()


def exchange(part, tile, params, first, second):
    width, groups = lax.axis_size("dp"), lax.axis_size("grp")
    rows = part.shape[0] // width
    half = width // 2
    inside = pl.BlockSpec(memory_space=pltpu.VMEM)
    outside = pl.BlockSpec(memory_space=pl.ANY)
    dma = pltpu.SemaphoreType.DMA
    many = [dma((PIECES,))] * 2
    fan = [dma((PIECES, half - 1))] * 2
    whole, mean, total = pl.pallas_call(
        lambda *refs: exchange_kernel(width, groups, params.shape[0], *refs),
        out_shape=[
            jax.ShapeDtypeStruct((width, rows, LANES), BF16),
            jax.ShapeDtypeStruct((width, rows, LANES), BF16),
            jax.ShapeDtypeStruct((24, LANES), F32),
        ],
        in_specs=[inside, inside, outside, outside, outside],
        out_specs=[inside, inside, inside],
        scratch_shapes=[
            pltpu.VMEM((half, rows, LANES), BF16),
            pltpu.VMEM((half, rows, LANES), BF16),
            pltpu.VMEM((half - 1, rows, LANES), BF16),
            pltpu.VMEM((rows, LANES), F32),
            pltpu.VMEM((rows, LANES), F32),
            pltpu.VMEM((rows, LANES), F32),
            pltpu.VMEM((rows, LANES), BF16),
            pltpu.VMEM((groups - 1, rows // groups, LANES), BF16),
            pltpu.VMEM((2, 16, LANES), F32),
            pltpu.VMEM((half, 16, LANES), F32),
        ]
        + [dma] * 3
        + many
        + fan
        + fan
        + many
        + [dma] * 2
        + [dma((half - 1,))] * 2
        + [dma((PIECES, groups - 1))] * 2
        + fan
        + many
        + [dma((PIECES, 2))] * 4,
        compiler_params=pltpu.CompilerParams(
            collective_id=1, has_side_effects=True, vmem_limit_bytes=VMEM_LIMIT
        ),
    )(part.reshape(width, rows, LANES), tile, params, first, second)
    return whole.reshape(width * rows, LANES), mean.reshape(width * rows, LANES), total


def adamw_update(gradient_sum, factor, start, first, second):
    clipped = gradient_sum * factor
    new_first = BETA_ONE * first + (1.0 - BETA_ONE) * clipped
    new_second = BETA_TWO * second + (1.0 - BETA_TWO) * clipped * clipped
    corrected = (
        new_first
        / (1.0 - BETA_ONE**STEP_COUNT)
        / (jnp.sqrt(new_second / (1.0 - BETA_TWO**STEP_COUNT)) + EPSILON)
    )
    return (RATE_INNER * (corrected + WEIGHT_DECAY * start), new_first, new_second)


def outer_step(average, start, momentum):
    new_momentum = MOMENTUM_OUTER * momentum + average
    return (start - OUTER_RATE * (average + MOMENTUM_OUTER * new_momentum), new_momentum)


def local(
    images, noise, timesteps, counts, teacher, params, first_moment, second_moment, outer_momentum
):
    width = lax.axis_size("dp")
    part, tile = local_gradient(images, noise, timesteps, counts, teacher, params, width)
    start, first, second, momentum = lax.optimization_barrier(
        tuple(
            array.reshape(-1, LANES)
            for array in (params, first_moment, second_moment, outer_momentum)
        )
    )
    total, mean, scalars = exchange(part, tile, start, first, second)
    count = start.shape[0]
    _, new_first, new_second = adamw_update(
        total[:count].astype(F32), scalars[16, 0], start, first, second
    )
    average = mean[:count].astype(F32)
    new_weights, new_outer = outer_step(average, start, momentum)
    return (
        new_weights.reshape(-1),
        new_first.reshape(1, -1),
        new_second.reshape(1, -1),
        average.reshape(-1),
        new_outer.reshape(-1),
        scalars[0, 0:1],
        scalars[1, 0:1],
        scalars[8, 0:1],
    )


def solution(mesh):
    placed = (
        P(None, ("grp", "dp"), None, None, None),
        P(None, ("grp", "dp"), None, None, None),
        P(None, ("grp", "dp")),
        P(("grp", "dp"), None),
        P(),
        P(),
        P("grp", None),
        P("grp", None),
        P(),
    )
    return jax.shard_map(
        local,
        mesh=mesh,
        in_specs=placed,
        out_specs=(P(), P("grp", None), P("grp", None), P(), P(), P("grp"), P("grp"), P("grp")),
        check_vma=False,
    )
```

```python
import math
from types import SimpleNamespace

import jax
import jax.numpy as jnp
from jax import lax
from jax.experimental import pallas as pl
from jax.experimental.pallas import tpu as pltpu
from jax.sharding import PartitionSpec as P

BASE = 128
WIDE = 256
TEMB = 512
FREQ = 128
GROUPS = 32
STEPS = 64
STEP_COUNT = 10

BETA_ONE = 0.9
BETA_TWO = 0.999
EPSILON = 1e-08
RATE_INNER = 0.03
WEIGHT_DECAY = 0.01
CLIP_NORM = 0.005
OUTER_RATE = 0.7
MOMENTUM_OUTER = 0.9

F32 = jnp.float32
BF16 = jnp.bfloat16
LANES = 128
HALF = 16
PIX = HALF * HALF
VMEM_LIMIT = 60 * 1024 * 1024
EXCHANGE_LIMIT = 26 * 1024 * 1024
MESH = pl.DeviceIdType.MESH
PIECES = 5
UNIT = 320


SIZES = dict(
    conv_in=BASE * 27,
    bias_in=BASE,
    conv_down=WIDE * BASE * 9,
    bias_down=WIDE,
    norm_one_gain=WIDE,
    norm_one_shift=WIDE,
    conv_one=WIDE * WIDE * 9,
    bias_one=WIDE,
    time_one=FREQ * TEMB,
    time_bias_one=TEMB,
    time_two=TEMB * WIDE,
    time_bias_two=WIDE,
    norm_two_gain=WIDE,
    norm_two_shift=WIDE,
    conv_two=WIDE * WIDE * 9,
    bias_two=WIDE,
    attn_gain=WIDE,
    attn_shift=WIDE,
    attn_inner=WIDE * 3 * WIDE,
    attn_outer=WIDE * WIDE,
    attn_bias=WIDE,
    conv_up=BASE * WIDE * 9,
    bias_up=BASE,
    norm_out_gain=BASE,
    norm_out_shift=BASE,
    conv_out=3 * BASE * 9,
    bias_out=3,
)


def layout():
    return list(SIZES.items())


def start_rows():
    found = {}
    offset = 0
    for name, number in layout():
        found[name] = offset // LANES
        offset += number
    return SimpleNamespace(**found)


ROW = start_rows()
VECTOR_PLACES = dict(
    bias_in=0,
    bias_down=1,
    norm_one_gain=2,
    norm_one_shift=3,
    bias_one=4,
    time_bias_two=5,
    norm_two_gain=6,
    norm_two_shift=7,
    bias_two=8,
    attn_gain=9,
    attn_shift=10,
    attn_bias=11,
    bias_up=12,
    norm_out_gain=13,
    norm_out_shift=14,
)
VEC = SimpleNamespace(**VECTOR_PLACES)
VECTORS = [(place, getattr(ROW, name), SIZES[name] == BASE) for name, place in VECTOR_PLACES.items()]
JOINT = {(0, 0): (0,), (0, 1): (1, 2), (1, 0): (0, 1), (1, 1): (2,)}

PREP_SHAPES = dict(
    down=(3, 3 * BASE, WIDE),
    one=(3, 3 * WIDE, WIDE),
    two=(3, 3 * WIDE, WIDE),
    inner=(WIDE, 3 * WIDE),
    outer=(WIDE, WIDE),
    up=(4, 3 * WIDE, WIDE),
    time_one=(FREQ, TEMB),
    time_two=(TEMB, WIDE),
)
BACK_SHAPES = dict(
    down_t=(3, 2 * WIDE, WIDE),
    one_t=(3, 3 * WIDE, WIDE),
    two_t=(3, 3 * WIDE, WIDE),
    up_t=(4, 2 * WIDE, WIDE),
)


NN = (((1,), (0,)), ((), ()))
NT = (((1,), (1,)), ((), ()))
TN = (((0,), (0,)), ((), ()))


def product(left, right, kind):
    return lax.dot_general(left, right, kind, preferred_element_type=F32)


def dot(left, right):
    return product(left, right, NN)


def narrow_places():
    begin = 27 * lax.broadcasted_iota(jnp.int32, (32, LANES), 1)
    row = lax.broadcasted_iota(jnp.int32, (32, LANES), 0)
    low = jnp.where(begin // LANES == row, 1.0, 0.0)
    high = jnp.where(begin // LANES + 1 == row, 1.0, 0.0)
    offset = (27 * lax.broadcasted_iota(jnp.int32, (LANES, LANES), 0)) % LANES
    lane = lax.broadcasted_iota(jnp.int32, (LANES, LANES), 1)
    return low, high, offset, lane >= offset


def roll_rows(values, offset, sign):
    for bit in range(7):
        moved = pltpu.roll(values, (sign << bit) % LANES, axis=1)
        values = jnp.where((offset >> bit) % 2 == 1, moved, values)
    return values


def prep_kernel(with_back, rows, *refs):
    if rows.dtype == BF16:
        rows, low, refs = refs[-1], rows, refs[:-1]
        step = low.shape[0] // 256 * 16

        def widen(index, carry):
            block = pl.ds(pl.multiple_of(index * step, 16), step)
            rows[block, :] = low[block, :].astype(F32)
            return carry

        lax.fori_loop(0, 16, widen, 0)
        rows[16 * step :, :] = low[16 * step :, :].astype(F32)
    names = list(PREP_SHAPES) + (list(BACK_SHAPES) if with_back else [])
    out = SimpleNamespace(**dict(zip(names, refs)))
    enter, leave, bias_out, vec, bias_hidden, turned, square, taps = refs[len(names) :]

    def turn(start, wide_out, wide_in):
        count = wide_in * 9 // LANES
        for b in range(count):
            block = rows[pl.ds(start + b, wide_out, stride=count), :].T
            for c in range(0, wide_out, LANES):
                turned[c // LANES, b * LANES : (b + 1) * LANES, :] = block[:, c : c + LANES]

    def tap(k, wide_out, wide_in):
        parts = [turned[c, pl.ds(k, wide_in, stride=9), :] for c in range(wide_out // LANES)]
        return parts[0] if len(parts) == 1 else jnp.concatenate(parts, axis=1)

    for start, place, place_t in (
        (ROW.conv_one, out.one, out.one_t if with_back else None),
        (ROW.conv_two, out.two, out.two_t if with_back else None),
    ):
        turn(start, WIDE, WIDE)
        for ky in range(3):
            for kx in range(3):
                block = tap(3 * ky + kx, WIDE, WIDE)
                place[ky, kx * WIDE : (kx + 1) * WIDE, :] = block.astype(BF16)
                if with_back:
                    place_t[ky, kx * WIDE : (kx + 1) * WIDE, :] = block.T.astype(BF16)
    turn(ROW.conv_down, WIDE, BASE)
    for ky in range(3):
        for kx in range(3):
            block = tap(3 * ky + kx, WIDE, BASE)
            out.down[ky, kx * BASE : (kx + 1) * BASE, :] = block.astype(BF16)
            if with_back:
                back = block.T.astype(BF16)
                if kx == 0:
                    out.down_t[ky, 0:WIDE, BASE:] = back
                elif kx == 1:
                    out.down_t[ky, 0:WIDE, 0:BASE] = jnp.zeros((WIDE, BASE), BF16)
                    out.down_t[ky, WIDE:, 0:BASE] = back
                else:
                    out.down_t[ky, WIDE:, BASE:] = back
    turn(ROW.conv_up, BASE, WIDE)
    for py in range(2):
        for ty in range(2):
            index = 2 * py + ty
            for px in range(2):
                for tx in range(2):
                    total = None
                    for ky in JOINT[py, ty]:
                        for kx in JOINT[px, tx]:
                            term = tap(3 * ky + kx, BASE, WIDE).astype(BF16).astype(F32)
                            total = term if total is None else total + term
                    xo = px + tx
                    out.up[index, xo * WIDE : (xo + 1) * WIDE, px * BASE : (px + 1) * BASE] = (
                        total.astype(BF16)
                    )
                    if with_back:
                        at = (2 * px + tx) * BASE
                        out.up_t[index, at : at + BASE, :] = total.T.astype(BF16)
                at = 2 * WIDE if px == 0 else 0
                out.up[index, at : at + WIDE, px * BASE : (px + 1) * BASE] = jnp.zeros(
                    (WIDE, BASE), BF16
                )
    for start, place in (
        (ROW.attn_inner, out.inner),
        (ROW.attn_outer, out.outer),
        (ROW.time_one, out.time_one),
        (ROW.time_two, out.time_two),
    ):
        height, width = place.shape
        count = width // LANES
        for b in range(count):
            block = rows[pl.ds(start + b, height, stride=count), :]
            place[:, b * LANES : (b + 1) * LANES] = block.astype(BF16)
    vec[...] = jnp.zeros_like(vec)
    for place, r, narrow in VECTORS:
        second = r if narrow else r + 1
        vec[place : place + 1, 0:LANES] = rows[r : r + 1, :]
        vec[place : place + 1, LANES:] = rows[second : second + 1, :]
    for b in range(TEMB // LANES):
        r = ROW.time_bias_one + b
        bias_hidden[:, b * LANES : (b + 1) * LANES] = jnp.broadcast_to(rows[r : r + 1, :], (8, LANES))
    low, high, offset, upper_part = narrow_places()
    block = rows[0:32, :].astype(BF16)
    merged = jnp.where(
        upper_part, dot(low.T.astype(BF16), block), dot(high.T.astype(BF16), block)
    )
    merged = roll_rows(merged, offset, -1).T
    taps[...] = jnp.zeros_like(taps)
    for k in range(9):
        for c in range(3):
            taps[8 * k + c : 8 * k + c + 1, :] = merged[9 * c + k : 9 * c + k + 1, :]
    enter[...] = taps[...].astype(BF16)
    square[...] = jnp.zeros_like(square)
    for b in range(9):
        for c in range(3):
            at = ROW.conv_out + 9 * c + b
            square[c : c + 1, :] = rows[at : at + 1, :]
        turned[0, b * LANES : (b + 1) * LANES, :] = square[...].T
    for k in range(9):
        taps[8 * k : 8 * k + 8, :] = turned[0, pl.ds(k, LANES, stride=9), :].T[0:8, :]
    leave[...] = taps[...].astype(BF16)
    lane = lax.broadcasted_iota(jnp.int32, (8, LANES), 1)
    place = lax.broadcasted_iota(jnp.int32, (8, LANES), 0)
    chosen = jnp.logical_and(lane == place, place < 3)
    last = jnp.broadcast_to(rows[ROW.bias_out : ROW.bias_out + 1, :], (8, LANES))
    bias_out[...] = jnp.broadcast_to(
        jnp.sum(jnp.where(chosen, last, 0.0), axis=1, keepdims=True), (8, LANES)
    )


def prep_weights(flat, with_back):
    rows = flat.reshape(-1, LANES)
    shapes = dict(PREP_SHAPES)
    if with_back:
        shapes.update(BACK_SHAPES)
    whole = pl.BlockSpec(memory_space=pltpu.VMEM)
    made = pl.pallas_call(
        lambda *refs: prep_kernel(with_back, *refs),
        out_shape=[jax.ShapeDtypeStruct(s, BF16) for s in shapes.values()]
        + [
            jax.ShapeDtypeStruct((72, BASE), BF16),
            jax.ShapeDtypeStruct((72, BASE), BF16),
            jax.ShapeDtypeStruct((8, LANES), F32),
            jax.ShapeDtypeStruct((16, WIDE), F32),
            jax.ShapeDtypeStruct((8, TEMB), F32),
        ],
        in_specs=[whole],
        out_specs=[whole] * (len(shapes) + 5),
        scratch_shapes=[
            pltpu.VMEM((WIDE // LANES, 9 * WIDE, LANES), F32),
            pltpu.VMEM((LANES, LANES), F32),
            pltpu.VMEM((72, LANES), F32),
        ]
        + ([pltpu.VMEM(rows.shape, F32)] if rows.dtype == BF16 else []),
        compiler_params=pltpu.CompilerParams(vmem_limit_bytes=VMEM_LIMIT),
    )(rows)
    found = SimpleNamespace(**dict(zip(shapes, made)))
    found.enter, found.leave, found.bias_out, found.vec, found.bias_hidden = made[-5:]
    return found


def forward_set(found):
    return dict(
        {name: getattr(found, name) for name in PREP_SHAPES},
        vec=found.vec,
        bias_hidden=found.bias_hidden,
        enter=found.enter,
        leave=found.leave,
        bias_out=found.bias_out,
    )


def back_set(found):
    return {name: getattr(found, name) for name in BACK_SHAPES}


def move_x(values, distance):
    if distance == 0:
        return values
    column = lax.broadcasted_iota(jnp.int32, values.shape, 0) % HALF
    keep = column < HALF - 1 if distance > 0 else column >= 1
    rolled = pltpu.roll(values, (-distance) % values.shape[0], axis=0)
    return jnp.where(keep, rolled, 0.0)


def move_plane(values, ys, xs):
    if ys == 0 and xs == 0:
        return values
    lane = lax.broadcasted_iota(jnp.int32, values.shape, 1)
    row, column = lane // HALF, lane % HALF
    keep = None
    for place, step in ((row, ys), (column, xs)):
        if step:
            test = place < HALF - 1 if step > 0 else place >= 1
            keep = test if keep is None else jnp.logical_and(keep, test)
    rolled = pltpu.roll(values, (-(HALF * ys + xs)) % PIX, axis=1)
    return jnp.where(keep, rolled, 0.0)


def source_of(phase, step):
    return (phase + step) % 2, (phase + step) // 2


def silu_slope(values):
    gate = 1.0 / (1.0 + jnp.exp(-values))
    return gate * (1.0 + values * (1.0 - gate))


def silu(values):
    return values * (1.0 / (1.0 + jnp.exp(-values)))


def column_sum(values):
    return jnp.sum(values, axis=0, keepdims=True)


def group_sum(vectors, members):
    rest = 8 - len(vectors)
    stacked = jnp.concatenate(vectors + ([jnp.zeros((rest, WIDE), F32)] if rest else []), axis=0)
    high = stacked.astype(BF16).astype(F32)
    rest = stacked - high
    middle = rest.astype(BF16).astype(F32)
    parts = jnp.concatenate([high, middle, rest - middle, jnp.zeros_like(high)], axis=0)
    summed = dot(parts.astype(BF16), members[...])
    total = summed[0:8] + summed[8:16] + summed[16:24]
    return [total[i : i + 1] for i in range(len(vectors))]


NORM_WIDE = PIX * (WIDE // GROUPS)
NORM_BASE = 4 * PIX * (BASE // GROUPS)


def network_kernel(images_here, stream_count, given, made, scratch, own, *refs):
    teach, learn, r = SimpleNamespace(), SimpleNamespace(), SimpleNamespace()
    owners = [r] * len(given[0]) + [teach] * len(given[1]) + [learn] * len(given[2])
    owners += [r] * (len(made) + len(scratch))
    names = list(given[0]) + list(given[1]) + list(given[2]) + list(made) + list(scratch)
    streams = []
    for _ in range(stream_count):
        streams.append(SimpleNamespace())
        owners += [streams[-1]] * len(own)
        names += list(own)
    for owner, name, ref in zip(owners, names, refs, strict=True):
        setattr(owner, name, ref)
    wide, base = r.members_wide, r.members_base
    once = images_here == stream_count

    lane = lax.broadcasted_iota(jnp.int32, (WIDE, WIDE), 1)
    row = lax.broadcasted_iota(jnp.int32, (WIDE, WIDE), 0)
    per_wide, per_base = WIDE // GROUPS, BASE // GROUPS
    wide[...] = jnp.where(lane // per_wide == row // per_wide, 1.0, 0.0).astype(BF16)
    base[...] = jnp.where(
        (lane % BASE) // per_base == (row % BASE) // per_base, 1.0, 0.0
    ).astype(BF16)
    for q in streams:
        for ref in (q.cat_down, q.cat, q.cat_up):
            ref[...] = jnp.zeros_like(ref)
    for ref in (r.acc_vec, r.small, r.hidden_low, r.grad_shift):
        ref[...] = jnp.zeros_like(ref)
    totals = (r.acc_down, r.acc_one, r.acc_two, r.acc_up, r.acc_inner, r.acc_outer)
    if not once:
        for ref in totals + (r.grad_in, r.grad_out):
            ref[...] = jnp.zeros_like(ref)

    def vector(who, place):
        return who.vec[place : place + 1, :]

    def add_vector(place, value):
        r.acc_vec[place : place + 1, :] += value

    def time_path(who, embed, shift_ref, keep):
        pre = dot(embed[...].astype(BF16), who.time_one[...]) + who.bias_hidden[...]
        hidden = silu(pre)
        shift_ref[...] = dot(hidden.astype(BF16), who.time_two[...]) + vector(who, VEC.time_bias_two)
        if keep:
            r.hidden[...] = pre
            r.hidden_low[0:8, :] = hidden

    time_path(teach, r.embed_one, r.shift_t1, False)
    time_path(teach, r.embed_two, r.shift_t2, False)
    time_path(learn, r.embed_one, r.shift_s, True)

    def rows_product(pairs, kind=NN):
        return SimpleNamespace(answer=answer_rows, pairs=pairs, kind=kind)

    def answer_rows(asked):
        total = None
        for index, (_, right) in enumerate(asked[0].pairs):
            lefts = [ask.pairs[index][0] for ask in asked]
            left = jnp.concatenate(lefts, axis=1 if asked[0].kind is TN else 0)
            term = product(left, right[...], asked[0].kind)
            total = term if total is None else total + term
        return jnp.split(total, len(asked), axis=0)

    def lanes_product(left, right):
        return SimpleNamespace(answer=answer_lanes, left=left, right=right)

    def answer_lanes(asked):
        right = jnp.concatenate([ask.right for ask in asked], axis=0)
        return jnp.split(product(asked[0].left[...], right, NT), len(asked), axis=1)

    def add_product(target, place, left, right, kind=TN):
        return SimpleNamespace(
            answer=answer_total, target=target, place=place, left=left, right=right, kind=kind
        )

    def answer_total(asked):
        ask = asked[0]
        left = jnp.concatenate([a.left for a in asked], axis=0 if ask.kind is TN else 1)
        right = jnp.concatenate([a.right for a in asked], axis=0)
        total = product(left, right, ask.kind)
        if once and ask.opens:
            ask.target[ask.place] = total
        else:
            ask.target[ask.place] += total
        return [None] * len(asked)

    def group_sums(vectors, members):
        return SimpleNamespace(answer=answer_sums, vectors=vectors, members=members)

    def answer_sums(asked):
        count = len(asked[0].vectors)
        every = [vector_ for ask in asked for vector_ in ask.vectors]
        found = group_sum(every, asked[0].members)
        return [found[count * i : count * (i + 1)] for i in range(len(asked))]

    def norm_stats(blocks, members, count):
        total = sum(column_sum(block[...]) for block in blocks)
        (mean,) = yield group_sums([total], members)
        mean = mean * (1.0 / count)
        square = None
        for block in blocks:
            off = block[...] - mean
            term = column_sum(off * off)
            square = term if square is None else square + term
        (spread,) = yield group_sums([square], members)
        return mean, lax.rsqrt(spread * (1.0 / count) + 1e-05)

    def norm_back(grads, hats, gain, scale, members, count):
        plain = sum(column_sum(grad) for grad in grads)
        weighted = sum(column_sum(grad * hat) for grad, hat in zip(grads, hats))
        mean_plain, mean_weighted = yield group_sums([plain * gain, weighted * gain], members)
        mean_plain = mean_plain * (1.0 / count)
        mean_weighted = mean_weighted * (1.0 / count)
        inputs = [
            scale * (grad * gain - mean_plain - hat * mean_weighted)
            for grad, hat in zip(grads, hats)
        ]
        return inputs, weighted, plain

    def image_stream(q, index):
        taps, taps_back, first = q.taps, q.taps_back, q.first
        cat_down, cat, cat_up, joined, upper = q.cat_down, q.cat, q.cat_up, q.joined, q.upper
        body = slice(HALF, HALF + PIX)

        def set_taps(plane, sign, target):
            quarters = [plane[:, p * PIX : (p + 1) * PIX] for p in range(4)]
            for py in range(2):
                for px in range(2):
                    p = 2 * py + px
                    blocks = []
                    for ky in range(3):
                        for kx in range(3):
                            sy, ys = source_of(py, sign * (ky - 1))
                            sx, xs = source_of(px, sign * (kx - 1))
                            blocks.append(move_plane(quarters[2 * sy + sx], ys, xs))
                    target[:, p * PIX : (p + 1) * PIX] = jnp.concatenate(blocks, axis=0).astype(BF16)

        def set_cat(values):
            for kx in range(3):
                cat[body, kx * WIDE : (kx + 1) * WIDE] = move_x(values, kx - 1).astype(BF16)

        def convolve(kernel):
            return rows_product(
                [(cat[ky * HALF : ky * HALF + PIX, :], kernel.at[ky]) for ky in range(3)]
            )

        def make_plane():
            height = 3 * 2 * HALF
            rows = pl.ds(index * height, height) if isinstance(index, int) else pl.ds(
                pl.multiple_of(index * height, height), height
            )
            noisy = r.coef[index, 6] * r.images[rows, :] + r.coef[index, 7] * r.noise[rows, :]
            x = lax.broadcasted_iota(jnp.int32, (2 * HALF, 2 * PIX), 0)
            lane = lax.broadcasted_iota(jnp.int32, (2 * HALF, 2 * PIX), 1)
            spread = jnp.where(x == 2 * (lane % HALF) + lane // PIX, 1.0, 0.0).astype(BF16)
            values = dot(noisy.astype(BF16), spread)
            y = lax.broadcasted_iota(jnp.int32, values.shape, 0) % (2 * HALF)
            lane = lax.broadcasted_iota(jnp.int32, values.shape, 1) % PIX
            kept = jnp.where(lane // HALF == y // 2, values, 0.0)
            halves = []
            for py in range(2):
                part = jnp.where(y % 2 == py, kept, 0.0)
                lines = [
                    column_sum(part[c * 2 * HALF : (c + 1) * 2 * HALF, :]) for c in range(3)
                ]
                halves.append(jnp.concatenate(lines + [jnp.zeros((5, 2 * PIX), F32)], axis=0))
            return jnp.concatenate(halves, axis=1)

        def forward(who, plane, shift, keep):
            set_taps(plane, 1, taps)
            yield
            bias = vector(who, VEC.bias_in)[:, 0:BASE]
            for py in range(2):
                for px in range(2):
                    p = 2 * py + px
                    found = yield rows_product(
                        [(taps[:, p * PIX : (p + 1) * PIX], who.enter)], TN
                    )
                    first[py, :, px * BASE : (px + 1) * BASE] = found + bias
            for py in range(2):
                even, odd = first[py, :, 0:BASE], first[py, :, BASE:]
                cat_down[py, HALF:, 0:BASE] = move_x(odd, -1).astype(BF16)
                cat_down[py, HALF:, BASE : 2 * BASE] = even.astype(BF16)
                cat_down[py, HALF:, 2 * BASE :] = odd.astype(BF16)
            found = yield rows_product(
                [
                    (cat_down[1, 0:PIX, :], who.down.at[0]),
                    (cat_down[0, HALF:, :], who.down.at[1]),
                    (cat_down[1, HALF:, :], who.down.at[2]),
                ]
            )
            q.down[...] = found + vector(who, VEC.bias_down)
            stats_one = yield from norm_stats([q.down], wide, NORM_WIDE)
            hat = (q.down[...] - stats_one[0]) * stats_one[1]
            branch = silu(hat * vector(who, VEC.norm_one_gain) + vector(who, VEC.norm_one_shift))
            set_cat(branch)
            if keep:
                q.one_low[...] = branch.astype(BF16)
            found = yield convolve(who.one)
            q.branch[...] = found + (vector(who, VEC.bias_one) + shift)
            stats_two = yield from norm_stats([q.branch], wide, NORM_WIDE)
            hat = (q.branch[...] - stats_two[0]) * stats_two[1]
            branch = silu(hat * vector(who, VEC.norm_two_gain) + vector(who, VEC.norm_two_shift))
            set_cat(branch)
            if keep:
                q.two_low[...] = branch.astype(BF16)
            found = yield convolve(who.two)
            q.middle[...] = q.down[...] + found + vector(who, VEC.bias_two)
            stats_attn = yield from norm_stats([q.middle], wide, NORM_WIDE)
            hat = (q.middle[...] - stats_attn[0]) * stats_attn[1]
            tokens = hat * vector(who, VEC.attn_gain) + vector(who, VEC.attn_shift)
            tokens = tokens.astype(BF16)
            if keep:
                q.tokens[...] = tokens
            found = yield rows_product([(tokens, who.inner)])
            joined[...] = found.astype(BF16)
            scores = product(joined[:, 0:WIDE], joined[:, WIDE : 2 * WIDE], NT) * (WIDE**-0.5)
            yield
            weights = jnp.exp(scores - jnp.max(scores, axis=1, keepdims=True))
            weights = weights / jnp.sum(weights, axis=1, keepdims=True)
            if keep:
                q.soft[...] = weights
            yield
            mixed = dot(weights.astype(BF16), joined[:, 2 * WIDE :]).astype(BF16)
            if keep:
                q.mixed[...] = mixed
            found = yield rows_product([(mixed, who.outer)])
            set_cat(q.middle[...] + (found + vector(who, VEC.attn_bias)))
            for py in range(2):
                found = yield rows_product(
                    [
                        (cat[low * HALF : low * HALF + PIX, :], who.up.at[py + low])
                        for low in (py, py + 1)
                    ]
                )
                upper[py] = found + vector(who, VEC.bias_up) + first[py]
            stats_out = yield from norm_stats([upper.at[0], upper.at[1]], base, NORM_BASE)
            replies = []
            for py in range(2):
                hat = (upper[py] - stats_out[0]) * stats_out[1]
                ending = silu(
                    hat * vector(who, VEC.norm_out_gain) + vector(who, VEC.norm_out_shift)
                ).astype(BF16)
                if keep:
                    q.end[py] = ending
                for px in range(2):
                    reply = yield lanes_product(who.leave, ending[:, px * BASE : (px + 1) * BASE])
                    replies.append(reply)
            outs = []
            for py in range(2):
                for px in range(2):
                    total = None
                    for ky in range(3):
                        for kx in range(3):
                            sy, ys = source_of(py, ky - 1)
                            sx, xs = source_of(px, kx - 1)
                            k = 3 * ky + kx
                            term = move_plane(replies[2 * sy + sx][8 * k : 8 * k + 8, :], ys, xs)
                            total = term if total is None else total + term
                    outs.append(total)
            guess = jnp.concatenate(outs, axis=1) + who.bias_out[:, 0:1]
            return guess, stats_one, stats_two, stats_attn, stats_out

        def conv_back(grad, acc, value, kernel):
            for kx in range(3):
                cat[body, kx * WIDE : (kx + 1) * WIDE] = move_x(grad, 1 - kx).astype(BF16)

            def block(ky):
                low = (2 - ky) * HALF
                return cat[low : low + PIX, :]

            found = yield rows_product([(block(ky), kernel.at[ky]) for ky in range(3)])
            for ky in range(3):
                yield add_product(acc, ky, value[...], block(ky))
            return found

        def silu_norm_back(grad, place, stats, values):
            gain = vector(learn, place)
            hat = (values - stats[0]) * stats[1]
            slope = silu_slope(hat * gain + vector(learn, place + 1))
            (back,), grad_gain, grad_bias = yield from norm_back(
                [grad * slope], [hat], gain, stats[1], wide, NORM_WIDE
            )
            add_vector(place, grad_gain)
            add_vector(place + 1, grad_bias)
            return back

        at = pl.ds(index, 1)
        coef = [r.coef[index, j] for j in range(5)]
        plane = make_plane()
        guess_one = (yield from forward(teach, plane, r.shift_t1[at, :], False))[0]
        middle_state = coef[0] * guess_one + coef[1] * plane
        guess_two = (yield from forward(teach, middle_state, r.shift_t2[at, :], False))[0]
        target = coef[2] * guess_one + coef[3] * guess_two
        guess, stats_one, stats_two, stats_attn, stats_out = yield from forward(
            learn, plane, r.shift_s[at, :], True
        )
        error = guess - target
        weight = coef[4] * (1.0 / (3 * 4 * PIX))
        loss = jnp.sum(jnp.sum(error * error, axis=1, keepdims=True), axis=0, keepdims=True)
        r.small[8:9, :] += jnp.broadcast_to(loss * weight, (1, LANES))
        grad_guess = (2.0 * weight) * error
        r.small[0:8, :] += jnp.broadcast_to(
            jnp.sum(grad_guess, axis=1, keepdims=True), (8, LANES)
        )
        set_taps(grad_guess, -1, taps_back)
        yield
        grads = []
        for py in range(2):
            parts = []
            for px in range(2):
                p = 2 * py + px
                part = yield rows_product(
                    [(taps_back[:, p * PIX : (p + 1) * PIX], learn.leave)], TN
                )
                parts.append(part)
            grads.append(jnp.concatenate(parts, axis=1))
        ends = [q.end[p // 2, :, (p % 2) * BASE : (p % 2 + 1) * BASE] for p in range(4)]
        yield add_product(
            r.grad_out, slice(None), taps_back[...], jnp.concatenate(ends, axis=0), NN
        )
        gain = vector(learn, VEC.norm_out_gain)
        hats = [(upper[py] - stats_out[0]) * stats_out[1] for py in range(2)]
        shift = vector(learn, VEC.norm_out_shift)
        grads = [grad * silu_slope(hat * gain + shift) for grad, hat in zip(grads, hats)]
        grads, grad_gain, grad_bias = yield from norm_back(
            grads, hats, gain, stats_out[1], base, NORM_BASE
        )
        add_vector(VEC.norm_out_gain, grad_gain)
        add_vector(VEC.norm_out_shift, grad_bias)
        add_vector(VEC.bias_up, column_sum(grads[0]) + column_sum(grads[1]))
        for py in range(2):
            upper[py] = grads[py]
            even, odd = grads[py][:, 0:BASE], grads[py][:, BASE:]
            cat_up[py, body, 0:BASE] = move_x(even, 1).astype(BF16)
            cat_up[py, body, BASE : 2 * BASE] = even.astype(BF16)
            cat_up[py, body, 2 * BASE : 3 * BASE] = odd.astype(BF16)
            cat_up[py, body, 3 * BASE :] = move_x(odd, -1).astype(BF16)
        blocks = []
        for place in range(4):
            py, low = place // 2, (2 - place // 2 - place % 2) * HALF
            blocks.append(cat_up[py, low : low + PIX, :])
        grad_middle = yield rows_product(
            [(block, learn.up_t.at[place]) for place, block in enumerate(blocks)]
        )
        for place in range(4):
            py, low = place // 2, (2 - place // 2 - place % 2) * HALF
            yield add_product(
                r.acc_up, place, cat[body, WIDE : 2 * WIDE], cat_up[py, low : low + PIX, :]
            )
        add_vector(VEC.attn_bias, column_sum(grad_middle))
        grad_low = grad_middle.astype(BF16)
        grad_mixed = yield rows_product([(grad_low, learn.outer)], NT)
        grad_mixed = grad_mixed.astype(BF16)
        yield add_product(r.acc_outer, slice(None), q.mixed[...], grad_low)
        soft = q.soft[...]
        grad_soft = product(grad_mixed, joined[:, 2 * WIDE :], NT)
        grad_value = product(soft.astype(BF16), grad_mixed, TN)
        yield
        grad_scores = soft * (grad_soft - jnp.sum(soft * grad_soft, axis=1, keepdims=True))
        grad_scores = grad_scores.astype(BF16)
        yield
        grad_query = dot(grad_scores, joined[:, WIDE : 2 * WIDE]) * (WIDE**-0.5)
        grad_key = product(grad_scores, joined[:, 0:WIDE], TN) * (WIDE**-0.5)
        joined[:, 0:WIDE] = grad_query.astype(BF16)
        joined[:, WIDE : 2 * WIDE] = grad_key.astype(BF16)
        joined[:, 2 * WIDE :] = grad_value.astype(BF16)
        grad_tokens = yield rows_product([(joined[...], learn.inner)], NT)
        yield add_product(r.acc_inner, slice(None), q.tokens[...], joined[...])
        hat = (q.middle[...] - stats_attn[0]) * stats_attn[1]
        (back,), grad_gain, grad_bias = yield from norm_back(
            [grad_tokens], [hat], vector(learn, VEC.attn_gain), stats_attn[1], wide, NORM_WIDE
        )
        add_vector(VEC.attn_gain, grad_gain)
        add_vector(VEC.attn_shift, grad_bias)
        grad_middle = grad_middle + back
        q.middle[...] = grad_middle
        add_vector(VEC.bias_two, column_sum(grad_middle))
        grad_branch = yield from conv_back(grad_middle, r.acc_two, q.two_low, learn.two_t)
        grad_branch = yield from silu_norm_back(
            grad_branch, VEC.norm_two_gain, stats_two, q.branch[...]
        )
        bias_grad = column_sum(grad_branch)
        add_vector(VEC.bias_one, bias_grad)
        add_vector(VEC.time_bias_two, bias_grad)
        r.grad_shift[at, :] = bias_grad
        grad_branch = yield from conv_back(grad_branch, r.acc_one, q.one_low, learn.one_t)
        back = yield from silu_norm_back(grad_branch, VEC.norm_one_gain, stats_one, q.down[...])
        grad_down = q.middle[...] + back
        add_vector(VEC.bias_down, column_sum(grad_down))
        cat[0:PIX, 0:WIDE] = move_x(grad_down, 1).astype(BF16)
        cat[0:PIX, WIDE : 2 * WIDE] = grad_down.astype(BF16)
        cat[PIX : PIX + HALF, :] = jnp.zeros((HALF, 3 * WIDE), BF16)
        here, below = slice(0, PIX), slice(HALF, HALF + PIX)
        pair = slice(0, 2 * WIDE)
        even = yield rows_product([(cat[here, pair], learn.down_t.at[1])])
        odd = yield rows_product(
            [(cat[below, pair], learn.down_t.at[0]), (cat[here, pair], learn.down_t.at[2])]
        )
        grads = [even + upper[0], odd + upper[1]]
        for ky, py, rows in ((0, 1, below), (1, 0, here), (2, 1, here)):
            yield add_product(r.acc_down, ky, cat_down[py, HALF:, BASE:], cat[rows, pair])
        if not once:
            cat[0:HALF, :] = jnp.zeros((HALF, 3 * WIDE), BF16)
        add_vector(VEC.bias_in, column_sum(grads[0]) + column_sum(grads[1]))
        ends = [
            grads[p // 2][:, (p % 2) * BASE : (p % 2 + 1) * BASE].astype(BF16) for p in range(4)
        ]
        yield add_product(r.grad_in, slice(None), taps[...], jnp.concatenate(ends, axis=0), NN)

    def images_step(step, carry):
        groups = []
        for begin in range(0, stream_count, 2):
            members = range(begin, min(begin + 2, stream_count))
            running = [image_stream(streams[i], step * stream_count + i) for i in members]
            groups.append(SimpleNamespace(opens=begin == 0, running=running, answers=[None] * 2))
        while groups:
            for group in list(groups):
                asked = []
                for stream, answer in zip(group.running, group.answers):
                    try:
                        asked.append(stream.send(answer))
                    except StopIteration:
                        pass
                if len(asked) < len(group.running):
                    groups.remove(group)
                elif asked[0] is None:
                    group.answers = [None] * len(asked)
                else:
                    asked[0].opens = group.opens
                    group.answers = asked[0].answer(asked)
        return carry

    if once:
        images_step(0, 0)
    else:
        lax.fori_loop(0, images_here // stream_count, images_step, 0)

    grad_shift = r.grad_shift[...].astype(BF16)
    grad_two = product(r.hidden_low[...].astype(BF16), grad_shift, TN)
    pre = r.hidden[...]
    grad_hidden = product(grad_shift, learn.time_two[...], NT)[0:8, :] * silu_slope(pre)
    grad_bias_hidden = column_sum(grad_hidden)
    pad = jnp.zeros((FREQ - 8, TEMB), F32)
    embed = jnp.concatenate([r.embed_one[...], pad[:, 0:FREQ]], axis=0)
    grad_one = product(
        embed.astype(BF16), jnp.concatenate([grad_hidden, pad], axis=0).astype(BF16), TN
    )

    flat, turned, square = r.flat, r.turned, r.square
    last = ROW.bias_out
    flat[last:, :] = jnp.zeros((flat.shape[0] - last, LANES), F32)
    square[...] = jnp.zeros_like(square)
    for k in range(9):
        for c in range(3):
            square[9 * c + k : 9 * c + k + 1, :] = r.grad_in[8 * k + c : 8 * k + c + 1, :]
    low, high, offset, upper_part = narrow_places()
    spread = roll_rows(square[...].T, offset, 1)
    flat[0:27, :] = (
        dot(low.astype(BF16), jnp.where(upper_part, spread, 0.0).astype(BF16))
        + dot(high.astype(BF16), jnp.where(upper_part, 0.0, spread).astype(BF16))
    )[0:27, :]
    square[...] = jnp.zeros_like(square)
    for k in range(9):
        square[0:8, :] = r.grad_out[8 * k : 8 * k + 8, :]
        turned[0, pl.ds(k, LANES, stride=9), :] = square[...].T
    for b in range(9):
        block = turned[0, b * LANES : (b + 1) * LANES, :].T
        for c in range(3):
            at = ROW.conv_out + 9 * c + b
            flat[at : at + 1, :] = block[c : c + 1, :]
    lane = lax.broadcasted_iota(jnp.int32, (8, LANES), 1)
    place = lax.broadcasted_iota(jnp.int32, (8, LANES), 0)
    flat[last : last + 1, :] = column_sum(jnp.where(lane == place, r.small[0:8, :], 0.0))
    count = r.coef[0, 5]
    for index in range(1, images_here):
        count = count + r.coef[index, 5]
    row = lax.broadcasted_iota(jnp.int32, (8, LANES), 0)
    loss = jnp.broadcast_to(r.small[8:9, :], (8, LANES))
    r.tile[...] = jnp.where(row == 0, loss, jnp.where(row == 1, count, 0.0))

    def unturn(start, wide_out, wide_in):
        count = wide_in * 9 // LANES
        for b in range(count):
            parts = [
                turned[c, b * LANES : (b + 1) * LANES, :].T for c in range(wide_out // LANES)
            ]
            block = parts[0] if len(parts) == 1 else jnp.concatenate(parts, axis=0)
            flat[pl.ds(start + b, wide_out, stride=count), :] = block

    def put_tap(k, value, wide_in):
        for c in range(0, value.shape[1], LANES):
            turned[c // LANES, pl.ds(k, wide_in, stride=9), :] = value[:, c : c + LANES]

    for start, acc in ((ROW.conv_one, r.acc_one), (ROW.conv_two, r.acc_two)):
        for ky in range(3):
            for kx in range(3):
                put_tap(3 * ky + kx, acc[ky, :, kx * WIDE : (kx + 1) * WIDE], WIDE)
        unturn(start, WIDE, WIDE)
    acc = r.acc_down
    for ky in range(3):
        put_tap(3 * ky, acc[ky, BASE:, 0:WIDE], BASE)
        put_tap(3 * ky + 1, acc[ky, 0:BASE, WIDE:], BASE)
        put_tap(3 * ky + 2, acc[ky, BASE:, WIDE:], BASE)
    unturn(ROW.conv_down, WIDE, BASE)
    acc = r.acc_up
    for ky in range(3):
        for kx in range(3):
            total = None
            for (py, ty), set_y in JOINT.items():
                for (px, tx), set_x in JOINT.items():
                    if ky in set_y and kx in set_x:
                        at = (2 * px + tx) * BASE
                        term = acc[2 * py + ty, :, at : at + BASE]
                        total = term if total is None else total + term
            put_tap(3 * ky + kx, total, WIDE)
    unturn(ROW.conv_up, BASE, WIDE)
    for start, value in (
        (ROW.attn_inner, r.acc_inner),
        (ROW.attn_outer, r.acc_outer),
        (ROW.time_one, grad_one),
        (ROW.time_two, grad_two),
    ):
        count = value.shape[1] // LANES
        for b in range(count):
            flat[pl.ds(start + b, value.shape[0], stride=count), :] = value[
                :, b * LANES : (b + 1) * LANES
            ]
    for place, at, narrow in VECTORS:
        low = r.acc_vec[place : place + 1, 0:LANES]
        high = r.acc_vec[place : place + 1, LANES:]
        if narrow:
            flat[at : at + 1, :] = low + high
        else:
            flat[at : at + 1, :] = low
            flat[at + 1 : at + 2, :] = high
    for b in range(TEMB // LANES):
        at = ROW.time_bias_one + b
        flat[at : at + 1, :] = grad_bias_hidden[:, b * LANES : (b + 1) * LANES]

    def narrow(index, carry):
        block = pl.ds(pl.multiple_of(index * UNIT, UNIT), UNIT)
        r.grad[block, :] = flat[block, :].astype(BF16)
        return carry

    lax.fori_loop(0, flat.shape[0] // UNIT, narrow, 0)


def network(images, noise, embed_one, embed_two, coef, teacher, student, row_count):
    images_here = coef.shape[0]
    whole = pl.BlockSpec(memory_space=pltpu.VMEM)
    tall = PIX + 2 * HALF
    given = (
        dict(coef=coef, images=images, noise=noise, embed_one=embed_one, embed_two=embed_two),
        forward_set(teacher),
        dict(forward_set(student), **back_set(student)),
    )
    made = dict(
        grad=((row_count, LANES), BF16),
        tile=((8, LANES), F32),
    )
    scratch = dict(
        members_wide=((WIDE, WIDE), BF16),
        members_base=((WIDE, WIDE), BF16),
        shift_t1=((8, WIDE), F32),
        shift_t2=((8, WIDE), F32),
        shift_s=((8, WIDE), F32),
        hidden=((8, TEMB), F32),
        hidden_low=((LANES, TEMB), F32),
        grad_shift=((LANES, WIDE), F32),
        acc_down=((3, WIDE, 2 * WIDE), F32),
        acc_one=((3, WIDE, 3 * WIDE), F32),
        acc_two=((3, WIDE, 3 * WIDE), F32),
        acc_up=((4, WIDE, 2 * WIDE), F32),
        acc_inner=((WIDE, 3 * WIDE), F32),
        acc_outer=((WIDE, WIDE), F32),
        acc_vec=((16, WIDE), F32),
        turned=((WIDE // LANES, 9 * WIDE, LANES), F32),
        grad_in=((72, LANES), F32),
        grad_out=((72, LANES), F32),
        small=((16, LANES), F32),
        square=((LANES, LANES), F32),
        flat=((row_count, LANES), F32),
    )
    own = dict(
        taps=((72, 4 * PIX), BF16),
        taps_back=((72, 4 * PIX), BF16),
        first=((2, PIX, WIDE), F32),
        cat_down=((2, PIX + HALF, 3 * BASE), BF16),
        cat=((tall, 3 * WIDE), BF16),
        cat_up=((2, tall, 2 * WIDE), BF16),
        down=((PIX, WIDE), F32),
        branch=((PIX, WIDE), F32),
        middle=((PIX, WIDE), F32),
        soft=((PIX, PIX), F32),
        joined=((PIX, 3 * WIDE), BF16),
        mixed=((PIX, WIDE), BF16),
        upper=((2, PIX, WIDE), F32),
        end=((2, PIX, WIDE), BF16),
        one_low=((PIX, WIDE), BF16),
        two_low=((PIX, WIDE), BF16),
        tokens=((PIX, WIDE), BF16),
    )
    stream_count = max(n for n in (4, 2, 1) if images_here % n == 0)
    arrays = [array for group in given for array in group.values()]
    specs = [whole] * len(arrays)
    specs[0] = pl.BlockSpec(memory_space=pltpu.SMEM)
    return pl.pallas_call(
        lambda *refs: network_kernel(
            images_here, stream_count, given, made, scratch, own, *refs
        ),
        out_shape=[jax.ShapeDtypeStruct(shape, kind) for shape, kind in made.values()],
        in_specs=specs,
        out_specs=[whole] * len(made),
        scratch_shapes=[
            pltpu.VMEM(shape, kind)
            for shape, kind in list(scratch.values()) + list(own.values()) * stream_count
        ],
        compiler_params=pltpu.CompilerParams(vmem_limit_bytes=VMEM_LIMIT),
    )(*arrays)


def chunk_rows(row_count, width):
    return -(-row_count // (width * UNIT)) * UNIT


def wave(times_now):
    half_freq = FREQ // 2
    freqs = jnp.exp(
        -math.log(10000.0) * jnp.arange(half_freq).astype(jnp.float32) / (half_freq - 1)
    )
    angles = 1000.0 * times_now[:, None] * freqs[None, :]
    return jnp.concatenate([jnp.sin(angles), jnp.cos(angles)], axis=1)


def local_gradient(images, noise, timesteps, counts, teacher, params, width):
    turns, slots = images.shape[0], images.shape[1]
    images_here = turns * slots
    times = (timesteps.astype(F32) / STEPS).reshape(images_here)
    times_mid = times - 0.5 / STEPS
    times_end = times - 1.0 / STEPS
    angle = 0.5 * math.pi
    alpha_now, sigma_now = jnp.cos(angle * times), jnp.sin(angle * times)
    sigma_mid, sigma_end = jnp.sin(angle * times_mid), jnp.sin(angle * times_end)
    step = math.pi / (4 * STEPS)
    slot_index = jnp.arange(slots, dtype=jnp.int32)
    valid = (slot_index[None, :] < counts[0][:, None]).astype(F32)
    weighting = valid.reshape(images_here) * (1.0 + (alpha_now / sigma_now) ** 2)
    coef = jnp.stack(
        [
            math.sin(step) / sigma_now,
            sigma_mid / sigma_now,
            sigma_end / (2.0 * math.cos(step) * sigma_mid),
            sigma_now / (2.0 * math.cos(step) * sigma_mid),
            weighting,
            valid.reshape(images_here),
            alpha_now,
            sigma_now,
        ],
        axis=1,
    )
    rows = ((0, 8 - images_here), (0, 0))
    embed_one, embed_two = jnp.pad(wave(times), rows), jnp.pad(wave(times_mid), rows)
    teacher_set = prep_weights(teacher, False)
    student_set = prep_weights(params, True)
    param_rows = params.shape[0] // LANES
    return network(
        images.reshape(-1, images.shape[-1]),
        noise.reshape(-1, noise.shape[-1]),
        embed_one,
        embed_two,
        coef,
        teacher_set,
        student_set,
        width * chunk_rows(param_rows, width),
    )


def remote(source, target, send, receive, place):
    return pltpu.make_async_remote_copy(
        src_ref=source,
        dst_ref=target,
        send_sem=send,
        recv_sem=receive,
        device_id=place,
        device_id_type=MESH,
    )


def greet(places):
    barrier = pltpu.get_barrier_semaphore()
    for place in places:
        pl.semaphore_signal(barrier, inc=1, device_id=place, device_id_type=MESH)
    pl.semaphore_wait(barrier, len(places))


def exchange_kernel(
    width, groups, param_rows, part, tile, params, first, second, whole, mean, total_tile, *rest
):
    near, partial, far, start, old_first, old_second, steps, quarter, tiles, sums = rest[0:10]
    held = rest[10:13]
    s_near, r_near, s_far, r_far, s_back, r_back, s_side, r_side = rest[13:21]
    s_tile, r_tile, s_sums, r_sums, s_step, r_step = rest[21:27]
    s_along, r_along, s_mean, r_mean, s_cross, r_cross, s_core, r_core = rest[27:35]
    chunk = part.shape[1]
    rows = chunk // PIECES
    share = chunk // groups
    share_rows = share // PIECES
    half = width // 2
    grp, me = lax.axis_index("grp"), lax.axis_index("dp")
    side, along = lax.rem(me, 2), me // 2
    beside = (grp, me + 1 - 2 * side)
    crossed = lax.rem(grp + groups // 2, groups)
    across = (crossed, me)
    twin = (grp + 1 - 2 * lax.rem(grp, 2), me)
    others = []
    for step in range(1, half):
        other = lax.rem(along + step, half)
        others.append((other, (grp, 2 * other + side)))
    peers = []
    for step in range(1, groups):
        peer = lax.rem(grp + step, groups)
        peers.append((peer, (peer, me)))
    slot = side * half + along
    mine, yours = side * half, (1 - side) * half
    greet([beside] + [place for _, place in others] + [place for _, place in peers])
    sent = []

    def send(source, target, semaphore, other_semaphore, place):
        copy = remote(source, target, semaphore, other_semaphore, place)
        copy.start()
        sent.append(copy)
        return copy

    def span(piece):
        return pl.ds(piece * rows, rows)

    first_leg = [
        send(
            part.at[pl.ds(yours, half), span(piece)],
            near.at[:, span(piece)],
            s_near.at[piece],
            r_near.at[piece],
            beside,
        )
        for piece in range(PIECES)
    ]

    full, tail = param_rows // chunk, param_rows % chunk
    pairs = ((params, start), (first, old_first), (second, old_second))

    def own_copies(count):
        at = pl.multiple_of(slot * chunk, 8)
        return [
            pltpu.make_async_copy(source.at[pl.ds(at, count)], target.at[0:count], held[i])
            for i, (source, target) in enumerate(pairs)
        ]

    for _, target in pairs:
        target[...] = jnp.zeros_like(target)

    @pl.when(slot < full)
    def _():
        copies = own_copies(chunk)
        for copy in copies:
            copy.start()
        for copy in copies:
            copy.wait()

    if tail:

        @pl.when(slot == full)
        def _():
            copies = own_copies(tail)
            for copy in copies:
                copy.start()
            for copy in copies:
                copy.wait()

    second_leg, third_leg, fourth_leg, squares = [], [], [], []

    def hand_on(piece):
        first_leg[piece].wait_recv()
        partial[:, span(piece)] = (
            part[pl.ds(mine, half), span(piece)].astype(F32) + near[:, span(piece)].astype(F32)
        ).astype(BF16)
        second_leg.append(
            [
                send(
                    partial.at[other, span(piece)],
                    far.at[index, span(piece)],
                    s_far.at[piece, index],
                    r_far.at[piece, index],
                    place,
                )
                for index, (other, place) in enumerate(others)
            ]
        )

    def finish(piece):
        total = part[slot, span(piece)].astype(F32) + near[along, span(piece)].astype(F32)
        for index, copy in enumerate(second_leg[piece]):
            copy.wait_recv()
            total = total + far[index, span(piece)].astype(F32)
        low = total.astype(BF16)
        whole[slot, span(piece)] = low
        low = low.astype(F32)
        squares.append(jnp.sum((low * low).reshape(-1, 8, LANES), axis=0))

    def give_back(piece):
        here = whole.at[slot, span(piece)]
        third_leg.append(
            [
                send(here, here, s_back.at[piece, index], r_back.at[piece, index], place)
                for index, (_, place) in enumerate(others)
            ]
        )

    def pass_aside(piece):
        for copy in third_leg[piece]:
            copy.wait_recv()
        here = whole.at[pl.ds(mine, half), span(piece)]
        fourth_leg.append(send(here, here, s_side.at[piece], r_side.at[piece], beside))

    leaving, gathered, sided, crossed_one, crossed_two, last, tile_copies = [], [], [], [], [], [], []

    def send_tiles():
        tiles[0, 0:8, :] = sum(squares[1:], squares[0])
        tiles[0, 8:16, :] = tile[...]
        copy = send(tiles.at[0], tiles.at[1], s_tile, r_tile, beside)
        copy.wait_recv()
        sums[along] = tiles[0] + tiles[1]
        for index, (_, place) in enumerate(others):
            tile_copies.append(
                send(sums.at[along], sums.at[along], s_sums.at[index], r_sums.at[index], place)
            )

    def share_span(owner, piece):
        return pl.ds(owner * share + piece * share_rows, share_rows)

    def step_adam():
        for copy in tile_copies:
            copy.wait_recv()
        summed = sums[0]
        for index in range(1, half):
            summed = summed + sums[index]
        square_total = jnp.sum(jnp.sum(summed[0:8], axis=1, keepdims=True), axis=0, keepdims=True)
        valid_total = summed[9:10, 0:1]
        norm_value = jnp.sqrt(square_total) / valid_total
        factor = CLIP_NORM / jnp.maximum(norm_value, CLIP_NORM) / valid_total
        total_tile[0:8, :] = summed[8:16]
        total_tile[8:16, :] = jnp.broadcast_to(norm_value, (8, LANES))
        total_tile[16:24, :] = jnp.broadcast_to(factor, (8, LANES))
        for begin in range(0, chunk, share):
            block = slice(begin, begin + share)
            diff = adamw_update(
                whole[slot, block].astype(F32),
                factor,
                start[block],
                old_first[block],
                old_second[block],
            )[0]
            steps[block] = diff.astype(BF16)
        for piece in range(PIECES):
            leaving.append(
                [
                    send(
                        steps.at[share_span(peer, piece)],
                        quarter.at[index, pl.ds(piece * share_rows, share_rows)],
                        s_step.at[piece, index],
                        r_step.at[piece, index],
                        place,
                    )
                    for index, (peer, place) in enumerate(peers)
                ]
            )

    def add_up(piece):
        total = steps[share_span(grp, piece)].astype(F32)
        for index, copy in enumerate(leaving[piece]):
            copy.wait_recv()
            total = total + quarter[index, pl.ds(piece * share_rows, share_rows)].astype(F32)
        mean[slot, share_span(grp, piece)] = (total * (1.0 / groups)).astype(BF16)
        here = mean.at[slot, share_span(grp, piece)]
        gathered.append(
            [
                send(here, here, s_along.at[piece, index], r_along.at[piece, index], place)
                for index, (_, place) in enumerate(others)
            ]
        )

    def pass_mean(piece):
        for copy in gathered[piece]:
            copy.wait_recv()
        here = mean.at[pl.ds(mine, half), share_span(grp, piece)]
        sided.append(send(here, here, s_mean.at[piece], r_mean.at[piece], beside))
        crossed_one.append(send(here, here, s_cross.at[piece, 0], r_cross.at[piece, 0], across))

    def pass_across(piece):
        sided[piece].wait_recv()
        here = mean.at[pl.ds(yours, half), share_span(grp, piece)]
        crossed_two.append(send(here, here, s_cross.at[piece, 1], r_cross.at[piece, 1], across))
        here = mean.at[:, share_span(grp, piece)]
        last.append(send(here, here, s_core.at[piece, 0], r_core.at[piece, 0], twin))

    def pass_twin(piece):
        crossed_one[piece].wait_recv()
        crossed_two[piece].wait_recv()
        here = mean.at[:, share_span(crossed, piece)]
        last.append(send(here, here, s_core.at[piece, 1], r_core.at[piece, 1], twin))

    h, f, g, a = hand_on, finish, give_back, pass_aside
    u, m, x, t = add_up, pass_mean, pass_across, pass_twin
    before = ((h, 0), (h, 1), (h, 2), (f, 0), (h, 3), (f, 1), (h, 4), (f, 2), (g, 0), (f, 3), (f, 4))
    after = ((g, 2), (u, 0), (u, 1), (a, 1), (m, 0), (u, 2), (m, 1), (x, 0), (g, 3), (a, 2), (u, 3))
    after += ((m, 2), (x, 1), (t, 0), (u, 4), (m, 3), (x, 2), (t, 1), (g, 4), (a, 3), (m, 4), (x, 3))
    after += ((t, 2), (x, 4), (t, 3), (t, 4), (a, 4))
    for stage, piece in before:
        stage(piece)
    send_tiles()
    give_back(1)
    pass_aside(0)
    step_adam()
    for stage, piece in after:
        stage(piece)
    for copy in fourth_leg + last:
        copy.wait_recv()
    for copy in sent:
        copy.wait_send()


def exchange(part, tile, params, first, second):
    width, groups = lax.axis_size("dp"), lax.axis_size("grp")
    rows = part.shape[0] // width
    half = width // 2
    inside = pl.BlockSpec(memory_space=pltpu.VMEM)
    outside = pl.BlockSpec(memory_space=pl.ANY)
    dma = pltpu.SemaphoreType.DMA
    many = [dma((PIECES,))] * 2
    fan = [dma((PIECES, half - 1))] * 2
    whole, mean, total = pl.pallas_call(
        lambda *refs: exchange_kernel(width, groups, params.shape[0], *refs),
        out_shape=[
            jax.ShapeDtypeStruct((width, rows, LANES), BF16),
            jax.ShapeDtypeStruct((width, rows, LANES), BF16),
            jax.ShapeDtypeStruct((24, LANES), F32),
        ],
        in_specs=[inside, inside, outside, outside, outside],
        out_specs=[inside, inside, inside],
        scratch_shapes=[
            pltpu.VMEM((half, rows, LANES), BF16),
            pltpu.VMEM((half, rows, LANES), BF16),
            pltpu.VMEM((half - 1, rows, LANES), BF16),
            pltpu.VMEM((rows, LANES), F32),
            pltpu.VMEM((rows, LANES), F32),
            pltpu.VMEM((rows, LANES), F32),
            pltpu.VMEM((rows, LANES), BF16),
            pltpu.VMEM((groups - 1, rows // groups, LANES), BF16),
            pltpu.VMEM((2, 16, LANES), F32),
            pltpu.VMEM((half, 16, LANES), F32),
        ]
        + [dma] * 3
        + many
        + fan
        + fan
        + many
        + [dma] * 2
        + [dma((half - 1,))] * 2
        + [dma((PIECES, groups - 1))] * 2
        + fan
        + many
        + [dma((PIECES, 2))] * 4,
        compiler_params=pltpu.CompilerParams(
            collective_id=1, has_side_effects=True, vmem_limit_bytes=EXCHANGE_LIMIT
        ),
    )(part.reshape(width, rows, LANES), tile, params, first, second)
    return whole.reshape(width * rows, LANES), mean.reshape(width * rows, LANES), total


def adamw_update(gradient_sum, factor, start, first, second):
    clipped = gradient_sum * factor
    new_first = BETA_ONE * first + (1.0 - BETA_ONE) * clipped
    new_second = BETA_TWO * second + (1.0 - BETA_TWO) * clipped * clipped
    corrected = (
        new_first
        / (1.0 - BETA_ONE**STEP_COUNT)
        / (jnp.sqrt(new_second / (1.0 - BETA_TWO**STEP_COUNT)) + EPSILON)
    )
    return (RATE_INNER * (corrected + WEIGHT_DECAY * start), new_first, new_second)


def outer_step(average, start, momentum):
    new_momentum = MOMENTUM_OUTER * momentum + average
    return (start - OUTER_RATE * (average + MOMENTUM_OUTER * new_momentum), new_momentum)


def local(
    images, noise, timesteps, counts, teacher, params, first_moment, second_moment, outer_momentum
):
    width = lax.axis_size("dp")
    part, tile = local_gradient(images, noise, timesteps, counts, teacher, params, width)
    start, first, second, momentum = lax.optimization_barrier(
        tuple(
            array.reshape(-1, LANES)
            for array in (params, first_moment, second_moment, outer_momentum)
        )
    )
    total, mean, scalars = exchange(part, tile, start, first, second)
    count = start.shape[0]
    _, new_first, new_second = adamw_update(
        total[:count].astype(F32), scalars[16, 0], start, first, second
    )
    average = mean[:count].astype(F32)
    new_weights, new_outer = outer_step(average, start, momentum)
    return (
        new_weights.reshape(-1),
        new_first.reshape(1, -1),
        new_second.reshape(1, -1),
        average.reshape(-1),
        new_outer.reshape(-1),
        scalars[0, 0:1],
        scalars[1, 0:1],
        scalars[8, 0:1],
    )


def solution(mesh):
    placed = (
        P(None, ("grp", "dp"), None, None, None),
        P(None, ("grp", "dp"), None, None, None),
        P(None, ("grp", "dp")),
        P(("grp", "dp"), None),
        P(),
        P(),
        P("grp", None),
        P("grp", None),
        P(),
    )
    return jax.shard_map(
        local,
        mesh=mesh,
        in_specs=placed,
        out_specs=(P(), P("grp", None), P("grp", None), P(), P(), P("grp"), P("grp"), P("grp")),
        check_vma=False,
    )
```
